512 devices in a mesh: fib: 128 (over y, z, core), run: 4 (over x).
Axes of the slice: x: 4, y: 4, z: 16, core: 2. Of those that a mesh axis runs over, the one named last changes fastest.
Arguments:
- slab: bfloat16 [4, 512, 16384], P('run', 'fib'), may hold values from -6 to 6
- chord_weight: float32 [512], P('fib'), may hold values from 0.3 to 3
- span_weight: float32 [256], replicated, may hold values from 0.1 to 1
- start: float32 [512, 64], replicated, may hold values from -6 to 6
Outputs:
- core_unfolding: bfloat16 [4, 4096, 256], P('run', 'fib')
The draws below stay inside these ranges and needn't reach their ends.
All inputs are finite; a program needn't handle non-finite values.
Results may differ from the reference program's by a relative error of at most 0.0048.
The reference program's roundings to bfloat16 on the way count: a program that leaves them out, or rounds other values in their place, can miss the bound.
Values may be sent and summed in bfloat16 or wider, within the bound.
No kernel may reach another device: no remote copies, remote signals or barrier semaphores. Data moves between devices by JAX's collectives and lax.ppermute only.
A program may use at most 64 MiB of HBM per device.

```python
import math
import jax
import jax.numpy as jnp
from jax import lax

C = 512
K = 64
RANK = 64
ITERS = 3
R = 4
S = 256


def steps_of(own_key, dims, pieces, least, high):
    factor_of, own = 1.0, jax.random.fold_in(own_key, 6)
    for dim, blocks in pieces:
        steps = jnp.exp(jax.random.uniform(jax.random.fold_in(own, dim), (blocks,), jnp.float32, least / len(pieces), high / len(pieces)))
        factor_of = factor_of * jnp.repeat(steps, dims[dim] // blocks).reshape([-1 if axis == dim else 1 for axis in range(len(dims))])
    return factor_of


def noise(rng, shape, spread, reach, split=(), dtype=jnp.bfloat16):
    array = jax.random.normal(rng, shape, jnp.float32) * spread
    if len(split) > 0:
        array = steps_of(rng, shape, split, -0.22, 0.18) * array
    return jnp.clip(array, min=-reach, max=reach).astype(dtype)


def setup_inputs(seed: int = 0) -> dict:
    key_of = jax.random.split(jax.random.key(seed), 5)
    return {
        "slab": noise(key_of[0], (R, C, S * K), 1.0, 6.0, ((0, 4), (1, 128))),
        "chord_weight": jnp.clip(jnp.exp(math.log(3.0) - 2.3025851 * jax.random.uniform(key_of[1], (C,), jnp.float32) ** steps_of(key_of[1], (C,), ((0, 128),), -0.2, 0.2)), 0.3, 3.0),
        "span_weight": jnp.clip(jnp.exp(jax.random.uniform(key_of[2], (S,), jnp.float32, math.log(0.1), math.log(1.0))), 0.1, 1.0),
        "start": noise(key_of[3], (C, RANK), 1.0, 6.0, (), jnp.float32),
    }


def weigh(block, chord_weight, span_weight, time_rank):
    stations = jnp.repeat(span_weight, time_rank)
    return (block.astype(jnp.float32) * chord_weight[:, None] * stations[None, :]).astype(jnp.bfloat16)

def orthonormal(matrix):
    small = jnp.dot(matrix.T.astype(jnp.float32), matrix.astype(jnp.float32), precision=lax.Precision.HIGHEST, preferred_element_type=jnp.float32)
    lower_tri = jnp.linalg.cholesky(small)
    return lax.linalg.triangular_solve(lower_tri, matrix, left_side=False, lower=True, transpose_a=True)

def reference(slab, chord_weight, span_weight, start):

    def accumulate(total, block):
        weighted = weigh(block, chord_weight, span_weight, K)
        return (total + jnp.dot(weighted.astype(jnp.float32), weighted.T.astype(jnp.float32), preferred_element_type=jnp.float32), None)
    gram, _ = lax.scan(accumulate, jnp.zeros((C, C), jnp.float32), slab)
    factor = start
    for iteration in range(ITERS):
        product = jnp.dot(gram.astype(jnp.float32), factor.astype(jnp.float32), precision=lax.Precision.HIGHEST, preferred_element_type=jnp.float32)
        factor = orthonormal(product)
    narrow = factor.astype(jnp.bfloat16)

    def contract(block):
        weighted = weigh(block, chord_weight, span_weight, K)
        core_block = jnp.dot(narrow.T.astype(jnp.float32), weighted.astype(jnp.float32), preferred_element_type=jnp.float32).astype(jnp.bfloat16)
        return core_block.reshape(RANK, S, K).transpose(0, 2, 1).reshape(RANK * K, S)
    return lax.map(contract, slab)
```

```python
import jax
import jax.numpy as jnp
from jax import lax
from jax.experimental import pallas as pl
from jax.experimental.pallas import tpu as pltpu
from jax.sharding import Mesh, PartitionSpec as P

K = 64
ITERS = 3
LANES = 128
HIGHEST = lax.Precision.HIGHEST
VMEM = pl.BlockSpec(memory_space=pltpu.VMEM)
FIB = ("y", "z", "core")
PLANE = ("y", "core", "run")
PAIRS = [(i, j) for i in range(4) for j in range(i, 4)]


def call(kernel, shape, dtype, scratch=()):
    return pl.pallas_call(
        kernel,
        out_shape=jax.ShapeDtypeStruct(shape, dtype),
        out_specs=VMEM,
        scratch_shapes=scratch,
        compiler_params=pltpu.CompilerParams(vmem_limit_bytes=32 * 1024 * 1024),
    )


def nn(a, b, precision=None):
    return lax.dot_general(
        a, b, (((1,), (0,)), ((), ())), precision=precision, preferred_element_type=jnp.float32
    )


def nt(a, b, precision=None):
    return lax.dot_general(
        a, b, (((1,), (1,)), ((), ())), precision=precision, preferred_element_type=jnp.float32
    )


def tn(a, b, precision=None):
    return lax.dot_general(
        a, b, (((0,), (0,)), ((), ())), precision=precision, preferred_element_type=jnp.float32
    )


def weigh_kernel(slab_ref, chord_ref, span_ref, out_ref):
    lane = lax.broadcasted_iota(jnp.int32, (1, LANES), 1)
    chord = chord_ref[...]
    for tile in range(out_ref.shape[0]):
        stations = jnp.where(
            lane < K, span_ref[tile : tile + 1, 0:1], span_ref[tile : tile + 1, 1:2]
        )
        block = slab_ref[0, :, tile * LANES : (tile + 1) * LANES].astype(jnp.float32)
        out_ref[tile] = (block * chord * stations).astype(jnp.bfloat16)


def gram_kernel(fibres_ref, out_ref):
    for at, (i, j) in enumerate(PAIRS):
        out_ref[at * 128 : (at + 1) * 128, :] = nt(
            fibres_ref[i * 128 : (i + 1) * 128, :], fibres_ref[j * 128 : (j + 1) * 128, :]
        )


def inverse_cholesky(small):
    n = small.shape[0]
    eye = lax.broadcasted_iota(jnp.int32, (n, n), 0) == lax.broadcasted_iota(jnp.int32, (n, n), 1)
    both = jnp.concatenate([small, eye.astype(jnp.float32)], axis=1)
    blocks = [both[8 * b : 8 * b + 8] for b in range(n // 8)]
    sub = lax.broadcasted_iota(jnp.int32, (8, 1), 0)
    lane = lax.broadcasted_iota(jnp.int32, (8, 2 * n), 1)
    for j in range(n):
        own, i = divmod(j, 8)
        row = blocks[own][i : i + 1]
        row = row * (1.0 / row[:, j : j + 1])
        for b in range(own, n // 8):
            column = blocks[b][:, j : j + 1]
            if b == own:
                if i == 7:
                    continue
                column = jnp.where(sub > i, column, 0.0)
            blocks[b] = blocks[b] - column * row
    rows = []
    for b in range(n // 8):
        pivot = jnp.sum(jnp.where(lane == sub + 8 * b, blocks[b], 0.0), axis=1, keepdims=True)
        rows.append(blocks[b][:, n:] * lax.rsqrt(pivot))
    return jnp.concatenate(rows, axis=0)


def factor_kernel(packed_ref, start_ref, fibres_ref, out_ref, gram_ref):
    for at, (i, j) in enumerate(PAIRS):
        block = packed_ref[at * 128 : (at + 1) * 128, :]
        gram_ref[i * 128 : (i + 1) * 128, j * 128 : (j + 1) * 128] = block
        if i != j:
            gram_ref[j * 128 : (j + 1) * 128, i * 128 : (i + 1) * 128] = block.T
    factor = start_ref[...]
    for _ in range(ITERS):
        product = nn(factor, gram_ref[...], HIGHEST)
        small = nt(product, product, HIGHEST)
        factor = nn(inverse_cholesky(small), product, HIGHEST)
    core = nn(factor.astype(jnp.bfloat16), fibres_ref[...])
    rank = core.shape[0]
    for half in range(2):
        low = core[:, half * 32 : half * 32 + 32]
        high = core[:, K + half * 32 : K + half * 32 + 32]
        out_ref[half * rank : (half + 1) * rank, :] = jnp.concatenate([low, high], axis=1).astype(
            jnp.bfloat16
        )


def unfold_kernel(parts_ref, out_ref):
    senders = parts_ref.shape[0]
    row = lax.broadcasted_iota(jnp.int32, (senders, 2 * senders), 0)
    station = lax.broadcasted_iota(jnp.int32, (senders, 2 * senders), 1)
    half = senders // 2
    pair = jnp.where(row < half, 2 * row, 2 * (row - half) + 1)
    out = None
    for parity in range(2):
        place = (station == 2 * pair + parity).astype(jnp.bfloat16)
        term = tn(parts_ref[:, parity * 32 : parity * 32 + 32], place)
        out = term if out is None else out + term
    out_ref[0] = out.astype(jnp.bfloat16)


def swap(array, axes):
    return lax.all_to_all(array, axes, 0, 0, tiled=True)


def sum_everywhere(packed):
    rows = packed.shape[0] // 32
    part = swap(packed.reshape(32, rows, LANES), PLANE).sum(0)
    deep = -(-rows // 16)
    part = jnp.pad(part, ((0, 16 * deep - rows), (0, 0))).reshape(16, deep, LANES)
    part = swap(part, "z").sum(0)
    part = swap(jnp.broadcast_to(part[None], (16, deep, LANES)), "z")
    part = part.reshape(16 * deep, LANES)[:rows]
    return swap(jnp.broadcast_to(part[None], (32, rows, LANES)), PLANE).reshape(packed.shape)


def per_device(slab, chord_weight, span_weight, start):
    rows, columns = slab.shape[1:]
    tiles = columns // LANES
    send = call(weigh_kernel, (tiles, rows, LANES), jnp.bfloat16)(
        slab, chord_weight[:, None], span_weight.reshape(tiles, 2)
    )
    fibres = swap(send, FIB).reshape(tiles * rows, LANES)
    packed = call(gram_kernel, (len(PAIRS) * 128, 128), jnp.float32)(fibres)
    packed = sum_everywhere(packed)
    chords, rank = start.shape
    parts = call(
        factor_kernel,
        (2 * rank, K),
        jnp.bfloat16,
        [pltpu.VMEM((chords, chords), jnp.float32)],
    )(packed, start.T, fibres)
    parts = swap(parts.reshape(2 * rank, 1, K), ("core", "y", "z")).reshape(2 * rank, K)
    return call(unfold_kernel, (1, 32, 2 * tiles), jnp.bfloat16)(parts)


def solution(mesh):
    fine = Mesh(mesh.devices.reshape(4, 16, 2, 4), FIB + ("run",))
    return jax.shard_map(
        per_device,
        mesh=fine,
        in_specs=(P("run", FIB, None), P(FIB), P(), P()),
        out_specs=P("run", FIB, None),
        check_vma=False,
    )
```

```python
import jax
import jax.numpy as jnp
from jax import lax
from jax.experimental import pallas as pl
from jax.experimental.pallas import tpu as pltpu
from jax.sharding import Mesh, PartitionSpec as P

K = 64
ITERS = 3
LANES = 128
HIGHEST = lax.Precision.HIGHEST
VMEM = pl.BlockSpec(memory_space=pltpu.VMEM)
SMEM = pl.BlockSpec(memory_space=pltpu.SMEM)
FIB = ("y", "z", "core")
PLANE = ("y", "core", "run")
PAIRS = [(i, j) for i in range(4) for j in range(i, 4)]


def call(kernel, shape, dtype, specs, scratch=()):
    return pl.pallas_call(
        kernel,
        out_shape=jax.ShapeDtypeStruct(shape, dtype),
        in_specs=specs,
        out_specs=VMEM,
        scratch_shapes=scratch,
        compiler_params=pltpu.CompilerParams(vmem_limit_bytes=32 * 1024 * 1024),
    )


def nn(a, b, precision=None):
    return lax.dot_general(
        a, b, (((1,), (0,)), ((), ())), precision=precision, preferred_element_type=jnp.float32
    )


def nt(a, b, precision=None):
    return lax.dot_general(
        a, b, (((1,), (1,)), ((), ())), precision=precision, preferred_element_type=jnp.float32
    )


def tn(a, b, precision=None):
    return lax.dot_general(
        a, b, (((0,), (0,)), ((), ())), precision=precision, preferred_element_type=jnp.float32
    )


def weigh_kernel(slab_ref, chord_ref, span_ref, out_ref):
    lane = lax.broadcasted_iota(jnp.int32, (1, LANES), 1)
    row = lax.broadcasted_iota(jnp.int32, (out_ref.shape[1], LANES), 0)
    chord = jnp.zeros(row.shape, jnp.float32)
    for i in range(out_ref.shape[1]):
        chord = jnp.where(row == i, chord_ref[i], chord)

    def weigh(tile):
        stations = jnp.where(lane < K, span_ref[2 * tile], span_ref[2 * tile + 1])
        block = slab_ref[0, :, tile * LANES : (tile + 1) * LANES].astype(jnp.float32)
        return block * chord * stations

    low_half = lane % K < K // 2
    for chip in range(out_ref.shape[0] // 2):
        first, second = weigh(2 * chip), weigh(2 * chip + 1)
        low = jnp.where(low_half, first, pltpu.roll(second, K // 2, 1))
        high = jnp.where(low_half, pltpu.roll(first, LANES - K // 2, 1), second)
        out_ref[2 * chip] = low.astype(jnp.bfloat16)
        out_ref[2 * chip + 1] = high.astype(jnp.bfloat16)


def gram_kernel(fibres_ref, out_ref):
    for at, (i, j) in enumerate(PAIRS):
        out_ref[at * 128 : (at + 1) * 128, :] = nt(
            fibres_ref[i * 128 : (i + 1) * 128, :], fibres_ref[j * 128 : (j + 1) * 128, :]
        )


def inverse_cholesky(small):
    n = small.shape[0]
    wide = (8, 2 * n)
    eye = lax.broadcasted_iota(jnp.int32, (n, n), 0) == lax.broadcasted_iota(jnp.int32, (n, n), 1)
    both = jnp.concatenate([small, eye.astype(jnp.float32)], axis=1)
    blocks = [both[8 * b : 8 * b + 8] for b in range(n // 8)]
    sub = lax.broadcasted_iota(jnp.int32, wide, 0)
    rows = []
    for own in range(n // 8):
        panel = [
            {
                b: jnp.broadcast_to(blocks[b][:, 8 * own + k : 8 * own + k + 1], wide)
                for b in range(own, n // 8)
            }
            for k in range(8)
        ]
        pivots = None
        for k in range(8):
            pivot = jnp.broadcast_to(panel[k][own][k : k + 1], wide)
            pivots = pivot if pivots is None else jnp.where(sub >= k, pivot, pivots)
            inverse = 1.0 / pivot
            row = jnp.broadcast_to(blocks[own][k : k + 1], wide) * inverse
            column = dict(panel[k])
            column[own] = jnp.where(sub > k, column[own], 0.0)
            for later in range(k + 1, 8):
                scale = jnp.broadcast_to(panel[later][own][k : k + 1], wide) * inverse
                for b in range(own, n // 8):
                    panel[later][b] = panel[later][b] - column[b] * scale
            for b in range(own, n // 8):
                blocks[b] = blocks[b] - column[b] * row
        rows.append(blocks[own][:, n:] * lax.rsqrt(pivots)[:, n:])
    return jnp.concatenate(rows, axis=0)


def factor_kernel(packed_ref, start_ref, fibres_ref, out_ref, gram_ref):
    for at, (i, j) in enumerate(PAIRS):
        block = packed_ref[at * 128 : (at + 1) * 128, :]
        gram_ref[i * 128 : (i + 1) * 128, j * 128 : (j + 1) * 128] = block
        if i != j:
            gram_ref[j * 128 : (j + 1) * 128, i * 128 : (i + 1) * 128] = block.T
    factor = start_ref[...]
    for _ in range(ITERS):
        product = nn(factor, gram_ref[...], HIGHEST)
        small = nt(product, product, HIGHEST)
        factor = nn(inverse_cholesky(small), product, HIGHEST)
    core = nn(factor.astype(jnp.bfloat16), fibres_ref[...])
    out_ref[...] = core.astype(jnp.bfloat16).astype(jnp.float32)


def unfold_kernel(parts_ref, out_ref):
    chips = parts_ref.shape[0]
    chip = lax.broadcasted_iota(jnp.int32, (chips, 4 * chips), 0)
    station = lax.broadcasted_iota(jnp.int32, (chips, 4 * chips), 1)
    parts = parts_ref[...].astype(jnp.bfloat16)
    out = None
    for at in range(4):
        place = (station == 4 * chip + at).astype(jnp.bfloat16)
        lane = K * (at % 2) + K // 2 * (at // 2)
        term = tn(parts[:, lane : lane + K // 2], place)
        out = term if out is None else out + term
    out_ref[0] = out.astype(jnp.bfloat16)


def swap(array, axes):
    return lax.all_to_all(array, axes, 0, 0, tiled=True)


def sum_everywhere(packed):
    rows = packed.shape[0] // 32
    part = swap(packed.reshape(32, rows, LANES), PLANE).sum(0)
    part = swap(jnp.broadcast_to(part[None], (16, rows, LANES)), "z").sum(0)
    return swap(jnp.broadcast_to(part[None], (32, rows, LANES)), PLANE).reshape(packed.shape)


def per_device(slab, chord_weight, span_weight, start):
    rows, columns = slab.shape[1:]
    tiles = columns // LANES
    send = call(weigh_kernel, (tiles, rows, LANES), jnp.bfloat16, [VMEM, SMEM, SMEM])(
        slab, chord_weight, span_weight
    )
    fibres = swap(send, FIB).reshape(tiles * rows, LANES)
    packed = call(gram_kernel, (len(PAIRS) * 128, 128), jnp.float32, [VMEM])(fibres)
    packed = sum_everywhere(packed)
    chords, rank = start.shape
    parts = call(
        factor_kernel,
        (rank, LANES),
        jnp.float32,
        [VMEM] * 3,
        [pltpu.VMEM((chords, chords), jnp.float32)],
    )(packed, start.T, fibres)
    parts = swap(parts.reshape(rank, 1, LANES), ("y", "z")).reshape(rank, LANES)
    return call(unfold_kernel, (1, K // 2, 4 * rank), jnp.bfloat16, [VMEM])(parts)


def solution(mesh):
    fine = Mesh(mesh.devices.reshape(4, 16, 2, 4), FIB + ("run",))
    return jax.shard_map(
        per_device,
        mesh=fine,
        in_specs=(P("run", FIB, None), P(FIB), P(), P()),
        out_specs=P("run", FIB, None),
        check_vma=False,
    )
```

```python
import jax
import jax.numpy as jnp
from jax import lax
from jax.experimental import pallas as pl
from jax.experimental.pallas import tpu as pltpu
from jax.sharding import Mesh, PartitionSpec as P

K = 64
ITERS = 3
LANES = 128
HIGHEST = lax.Precision.HIGHEST
VMEM = pl.BlockSpec(memory_space=pltpu.VMEM)
SMEM = pl.BlockSpec(memory_space=pltpu.SMEM)
CHIPS = ("y", "pair", "side")
FIB = CHIPS + ("core",)
PLANE = ("y", "run", "side")
PAIRS = [(i, j) for i in range(4) for j in range(i, 4)]


def call(kernel, shape, dtype, specs, scratch=()):
    return pl.pallas_call(
        kernel,
        out_shape=jax.ShapeDtypeStruct(shape, dtype),
        in_specs=specs,
        out_specs=VMEM,
        scratch_shapes=scratch,
        compiler_params=pltpu.CompilerParams(vmem_limit_bytes=32 * 1024 * 1024),
    )


def nn(a, b, precision=None):
    return lax.dot_general(
        a, b, (((1,), (0,)), ((), ())), precision=precision, preferred_element_type=jnp.float32
    )


def nt(a, b, precision=None):
    return lax.dot_general(
        a, b, (((1,), (1,)), ((), ())), precision=precision, preferred_element_type=jnp.float32
    )


def tn(a, b, precision=None):
    return lax.dot_general(
        a, b, (((0,), (0,)), ((), ())), precision=precision, preferred_element_type=jnp.float32
    )


def weigh_kernel(slab_ref, chord_ref, span_ref, out_ref):
    lane = lax.broadcasted_iota(jnp.int32, (1, LANES), 1)
    row = lax.broadcasted_iota(jnp.int32, (out_ref.shape[1], LANES), 0)
    chord = jnp.zeros(row.shape, jnp.float32)
    for i in range(out_ref.shape[1]):
        chord = jnp.where(row == i, chord_ref[i], chord)

    def weigh(tile):
        stations = jnp.where(lane < K, span_ref[2 * tile], span_ref[2 * tile + 1])
        block = slab_ref[0, :, tile * LANES : (tile + 1) * LANES].astype(jnp.float32)
        return block * chord * stations

    low_half = lane % K < K // 2
    for chip in range(out_ref.shape[0] // 2):
        first, second = weigh(2 * chip), weigh(2 * chip + 1)
        low = jnp.where(low_half, first, pltpu.roll(second, K // 2, 1))
        high = jnp.where(low_half, pltpu.roll(first, LANES - K // 2, 1), second)
        out_ref[2 * chip] = low.astype(jnp.bfloat16)
        out_ref[2 * chip + 1] = high.astype(jnp.bfloat16)


def gram_kernel(own_ref, other_ref, out_ref):
    core = lax.axis_index("core")
    for at in range(len(PAIRS) // 2):
        first, second = PAIRS[at], PAIRS[at + len(PAIRS) // 2]
        i, j = (
            pl.ds(pl.multiple_of(jnp.where(core == 0, low, high) * 128, 128), 128)
            for low, high in zip(first, second)
        )
        out_ref[at * 128 : (at + 1) * 128, :] = nt(own_ref[i, :], own_ref[j, :]) + nt(
            other_ref[i, :], other_ref[j, :]
        )


def inverse_cholesky(small):
    n = small.shape[0]
    wide = (8, 2 * n)
    eye = lax.broadcasted_iota(jnp.int32, (n, n), 0) == lax.broadcasted_iota(jnp.int32, (n, n), 1)
    both = jnp.concatenate([small, eye.astype(jnp.float32)], axis=1)
    blocks = [both[8 * b : 8 * b + 8] for b in range(n // 8)]
    sub = lax.broadcasted_iota(jnp.int32, wide, 0)
    rows = []
    for own in range(n // 8):
        panel = [
            {
                b: jnp.broadcast_to(blocks[b][:, 8 * own + k : 8 * own + k + 1], wide)
                for b in range(own, n // 8)
            }
            for k in range(8)
        ]
        pivots = None
        for k in range(8):
            pivot = jnp.broadcast_to(panel[k][own][k : k + 1], wide)
            pivots = pivot if pivots is None else jnp.where(sub >= k, pivot, pivots)
            inverse = 1.0 / pivot
            row = jnp.broadcast_to(blocks[own][k : k + 1], wide) * inverse
            column = dict(panel[k])
            column[own] = jnp.where(sub > k, column[own], 0.0)
            for later in range(k + 1, 8):
                scale = jnp.broadcast_to(panel[later][own][k : k + 1], wide) * inverse
                for b in range(own, n // 8):
                    panel[later][b] = panel[later][b] - column[b] * scale
            for b in range(own, n // 8):
                blocks[b] = blocks[b] - column[b] * row
        rows.append(blocks[own][:, n:] * lax.rsqrt(pivots)[:, n:])
    return jnp.concatenate(rows, axis=0)


def factor_kernel(own_ref, other_ref, start_ref, fibres_ref, out_ref, gram_ref):
    first = lax.axis_index("core") == 0
    for at, (i, j) in enumerate(PAIRS):
        rows = pl.ds(at % (len(PAIRS) // 2) * 128, 128)
        mine = first if at < len(PAIRS) // 2 else jnp.logical_not(first)
        block = jnp.where(mine, own_ref[rows, :], other_ref[rows, :])
        gram_ref[i * 128 : (i + 1) * 128, j * 128 : (j + 1) * 128] = block
        if i != j:
            gram_ref[j * 128 : (j + 1) * 128, i * 128 : (i + 1) * 128] = block.T
    product = nn(start_ref[...], gram_ref[...], HIGHEST)
    for iteration in range(ITERS):
        small = nt(product, product, HIGHEST)
        if iteration < ITERS - 1:
            product = nn(product, gram_ref[...], HIGHEST)
        product = nn(inverse_cholesky(small), product, HIGHEST)
    core = nn(product.astype(jnp.bfloat16), fibres_ref[...])
    out_ref[...] = core.astype(jnp.bfloat16).astype(jnp.float32)


def unfold_kernel(parts_ref, out_ref):
    chips = parts_ref.shape[0]
    chip = lax.broadcasted_iota(jnp.int32, (chips, 4 * chips), 0)
    station = lax.broadcasted_iota(jnp.int32, (chips, 4 * chips), 1)
    parts = parts_ref[...].astype(jnp.bfloat16)
    out = None
    for at in range(4):
        place = (station == 4 * chip + at).astype(jnp.bfloat16)
        lane = K * (at % 2) + K // 2 * (at // 2)
        term = tn(parts[:, lane : lane + K // 2], place)
        out = term if out is None else out + term
    out_ref[0] = out.astype(jnp.bfloat16)


def swap(array, axes):
    return lax.all_to_all(array, axes, 0, 0, tiled=True)


def to_other_core(array):
    return lax.ppermute(array, "core", [(0, 1), (1, 0)])


def sum_everywhere(packed):
    shards = 32
    shard = (packed.shape[0] // shards // 4, 4, LANES)
    part = swap(packed.reshape(shards, *shard), PLANE).sum(0)
    part = swap(jnp.broadcast_to(part[None], (8, *shard)), "pair").sum(0)
    return swap(jnp.broadcast_to(part[None], (shards, *shard)), PLANE).reshape(packed.shape)


def per_device(slab, chord_weight, span_weight, start):
    rows, columns = slab.shape[1:]
    tiles = columns // LANES
    send = call(weigh_kernel, (tiles, rows, LANES), jnp.bfloat16, [VMEM, SMEM, SMEM])(
        slab, chord_weight, span_weight
    )
    fibres = swap(send, FIB).reshape(tiles * rows, LANES)
    half = call(gram_kernel, (len(PAIRS) // 2 * 128, 128), jnp.float32, [VMEM] * 2)(
        fibres, to_other_core(fibres)
    )
    half = sum_everywhere(half)
    chords, rank = start.shape
    parts = call(
        factor_kernel,
        (rank, LANES),
        jnp.float32,
        [VMEM] * 4,
        [pltpu.VMEM((chords, chords), jnp.float32)],
    )(half, to_other_core(half), start.T, fibres)
    parts = swap(parts.reshape(rank, 1, LANES), CHIPS).reshape(rank, LANES)
    return call(unfold_kernel, (1, K // 2, 4 * rank), jnp.bfloat16, [VMEM])(parts)


def solution(mesh):
    fine = Mesh(mesh.devices.reshape(4, 8, 2, 2, 4), FIB + ("run",))
    return jax.shard_map(
        per_device,
        mesh=fine,
        in_specs=(P("run", FIB, None), P(FIB), P(), P()),
        out_specs=P("run", FIB, None),
        check_vma=False,
    )
```

```python
import jax
import jax.numpy as jnp
from jax import lax
from jax.experimental import pallas as pl
from jax.experimental.pallas import tpu as pltpu
from jax.sharding import Mesh, PartitionSpec as P

K = 64
ITERS = 3
LANES = 128
HIGHEST = lax.Precision.HIGHEST
VMEM = pl.BlockSpec(memory_space=pltpu.VMEM)
SMEM = pl.BlockSpec(memory_space=pltpu.SMEM)
CHIPS = ("y", "pair", "side")
PLANE = ("y", "run", "side")
PAIRS = [(0, 0), (0, 1), (1, 1), (0, 2), (1, 3), (2, 2), (2, 3), (3, 3), (2, 1), (3, 0)]


def call(kernel, shape, dtype, specs, scratch=()):
    return pl.pallas_call(
        kernel,
        out_shape=jax.ShapeDtypeStruct(shape, dtype),
        in_specs=specs,
        out_specs=VMEM,
        scratch_shapes=scratch,
        compiler_params=pltpu.CompilerParams(vmem_limit_bytes=32 * 1024 * 1024),
    )


def nn(a, b, precision=None):
    return lax.dot_general(
        a, b, (((1,), (0,)), ((), ())), precision=precision, preferred_element_type=jnp.float32
    )


def nt(a, b, precision=None):
    return lax.dot_general(
        a, b, (((1,), (1,)), ((), ())), precision=precision, preferred_element_type=jnp.float32
    )


def tn(a, b, precision=None):
    return lax.dot_general(
        a, b, (((0,), (0,)), ((), ())), precision=precision, preferred_element_type=jnp.float32
    )


def weigh_kernel(slab_ref, chord_ref, span_ref, out_ref):
    lane = lax.broadcasted_iota(jnp.int32, (1, LANES), 1)
    row = lax.broadcasted_iota(jnp.int32, (out_ref.shape[1], LANES), 0)
    chord = jnp.zeros(row.shape, jnp.float32)
    for i in range(out_ref.shape[1]):
        chord = jnp.where(row == i, chord_ref[i], chord)

    def weigh(tile):
        stations = jnp.where(lane < K, span_ref[2 * tile], span_ref[2 * tile + 1])
        block = slab_ref[0, :, tile * LANES : (tile + 1) * LANES].astype(jnp.float32)
        return block * chord * stations

    low_half = lane % K < K // 2
    for chip in range(out_ref.shape[0] // 2):
        first, second = weigh(2 * chip), weigh(2 * chip + 1)
        low = jnp.where(low_half, first, pltpu.roll(second, K // 2, 1))
        high = jnp.where(low_half, pltpu.roll(first, LANES - K // 2, 1), second)
        out_ref[2 * chip] = low.astype(jnp.bfloat16)
        out_ref[2 * chip + 1] = high.astype(jnp.bfloat16)


def gram_kernel(own_ref, other_ref, out_ref):
    first = lax.axis_index("core") == 0
    crossed = [(0, 2), (1, 3)]
    for at, (i, j) in enumerate([(0, 0), (0, 1), (1, 1), *crossed]):
        total = None
        for part in range(2):
            left = own_ref[part, i * 128 : (i + 1) * 128, :]
            if j < 2:
                right = own_ref[part, j * 128 : (j + 1) * 128, :]
            else:
                low, high = other_ref[part, :128, :], other_ref[part, 128:, :]
                right = jnp.where(first == (j == 2), low, high)
            term = nt(left, right)
            total = term if total is None else total + term
        out_ref[at * 128 : (at + 1) * 128, :] = total


def inverse_cholesky(small):
    n = small.shape[0]
    wide = (8, 2 * n)
    eye = lax.broadcasted_iota(jnp.int32, (n, n), 0) == lax.broadcasted_iota(jnp.int32, (n, n), 1)
    both = jnp.concatenate([small, eye.astype(jnp.float32)], axis=1)
    blocks = [both[8 * b : 8 * b + 8] for b in range(n // 8)]
    sub = lax.broadcasted_iota(jnp.int32, wide, 0)
    rows = []
    for own in range(n // 8):
        panel = [
            {
                b: jnp.broadcast_to(blocks[b][:, 8 * own + k : 8 * own + k + 1], wide)
                for b in range(own, n // 8)
            }
            for k in range(8)
        ]
        pivots = None
        for k in range(8):
            pivot = jnp.broadcast_to(panel[k][own][k : k + 1], wide)
            pivots = pivot if pivots is None else jnp.where(sub >= k, pivot, pivots)
            inverse = 1.0 / pivot
            row = jnp.broadcast_to(blocks[own][k : k + 1], wide) * inverse
            column = dict(panel[k])
            column[own] = jnp.where(sub > k, column[own], 0.0)
            for later in range(k + 1, 8):
                scale = jnp.broadcast_to(panel[later][own][k : k + 1], wide) * inverse
                for b in range(own, n // 8):
                    panel[later][b] = panel[later][b] - column[b] * scale
            for b in range(own, n // 8):
                blocks[b] = blocks[b] - column[b] * row
        rows.append(blocks[own][:, n:] * lax.rsqrt(pivots)[:, n:])
    return jnp.concatenate(rows, axis=0)


def factor_kernel(own_ref, other_ref, start_ref, own_fibres_ref, other_fibres_ref, out_ref, gram_ref):
    core = lax.axis_index("core")
    for at, (i, j) in enumerate(PAIRS):
        rows = pl.ds(at % 5 * 128, 128)
        mine = core == at // 5
        block = jnp.where(mine, own_ref[rows, :], other_ref[rows, :])
        gram_ref[i * 128 : (i + 1) * 128, j * 128 : (j + 1) * 128] = block
        if i != j:
            gram_ref[j * 128 : (j + 1) * 128, i * 128 : (i + 1) * 128] = block.T
    chords = gram_ref.shape[0]
    source = lax.broadcasted_iota(jnp.int32, (chords, chords), 0)
    target = lax.broadcasted_iota(jnp.int32, (chords, chords), 1)
    half = chords // 2
    wanted = target % half // 4 * 8 + target // half * 4 + target % 4
    order = (source == wanted).astype(jnp.bfloat16)
    rest = start_ref[...]
    start = jnp.zeros_like(rest)
    for _ in range(3):
        part = rest.astype(jnp.bfloat16)
        rest = rest - part.astype(jnp.float32)
        start = start + nn(part, order)
    product = nn(start, gram_ref[...], HIGHEST)
    for iteration in range(ITERS):
        small = nt(product, product, HIGHEST)
        if iteration < ITERS - 1:
            product = nn(product, gram_ref[...], HIGHEST)
        product = nn(inverse_cholesky(small), product, HIGHEST)
    narrow = product.astype(jnp.bfloat16)
    own = jnp.where(core == 0, own_fibres_ref[0], own_fibres_ref[1])
    other = jnp.where(core == 0, other_fibres_ref[0], other_fibres_ref[1])
    low, high = jnp.where(core == 0, own, other), jnp.where(core == 0, other, own)
    ranked = nn(narrow[:, :half], low) + nn(narrow[:, half:], high)
    out_ref[...] = ranked.astype(jnp.bfloat16).astype(jnp.float32)


def unfold_kernel(parts_ref, out_ref):
    chips = parts_ref.shape[0]
    chip = lax.broadcasted_iota(jnp.int32, (chips, 4 * chips), 0)
    station = lax.broadcasted_iota(jnp.int32, (chips, 4 * chips), 1)
    parts = parts_ref[...].astype(jnp.bfloat16)
    out = None
    for at in range(4):
        place = (station == 4 * chip + at).astype(jnp.bfloat16)
        lane = K * (at % 2) + K // 2 * (at // 2)
        term = tn(parts[:, lane : lane + K // 2], place)
        out = term if out is None else out + term
    out_ref[0] = out.astype(jnp.bfloat16)


def swap(array, axes):
    return lax.all_to_all(array, axes, 0, 0, tiled=True)


def to_other_core(array):
    return lax.ppermute(array, "core", [(0, 1), (1, 0)])


def sum_everywhere(packed):
    shards = 32
    shard = (packed.shape[0] // shards // 4, 4, LANES)
    part = swap(packed.reshape(shards, *shard), PLANE).sum(0)
    part = swap(jnp.broadcast_to(part[None], (8, *shard)), "pair").sum(0)
    return swap(jnp.broadcast_to(part[None], (shards, *shard)), PLANE).reshape(packed.shape)


def per_device(slab, chord_weight, span_weight, start):
    rows, columns = slab.shape[1:]
    tiles = columns // LANES
    send = call(weigh_kernel, (tiles, rows, LANES), jnp.bfloat16, [VMEM, SMEM, SMEM])(
        slab, chord_weight, span_weight
    )
    chips = tiles // 2
    received = swap(send.reshape(chips, 2, rows, LANES), CHIPS)
    own = received.transpose(1, 0, 2, 3).reshape(2, chips * rows, LANES)
    other = to_other_core(own)
    half = call(gram_kernel, (len(PAIRS) // 2 * 128, 128), jnp.float32, [VMEM] * 2)(own, other)
    half = sum_everywhere(half)
    chords, rank = start.shape
    parts = call(
        factor_kernel,
        (rank, LANES),
        jnp.float32,
        [VMEM] * 5,
        [pltpu.VMEM((chords, chords), jnp.float32)],
    )(half, to_other_core(half), start.T, own, other)
    parts = swap(parts.reshape(rank, 1, LANES), CHIPS).reshape(rank, LANES)
    return call(unfold_kernel, (1, K // 2, 4 * rank), jnp.bfloat16, [VMEM])(parts)


def solution(mesh):
    fine = Mesh(mesh.devices.reshape(4, 8, 2, 2, 4), CHIPS + ("core", "run"))
    return jax.shard_map(
        per_device,
        mesh=fine,
        in_specs=(P("run", CHIPS + ("core",), None), P(CHIPS + ("core",)), P(), P()),
        out_specs=P("run", CHIPS + ("core",), None),
        check_vma=False,
    )
```

```python
import jax
import jax.numpy as jnp
from jax import lax
from jax.experimental import pallas as pl
from jax.experimental.pallas import tpu as pltpu
from jax.sharding import Mesh, PartitionSpec as P

K = 64
ITERS = 3
LANES = 128
HIGHEST = lax.Precision.HIGHEST
VMEM = pl.BlockSpec(memory_space=pltpu.VMEM)
HBM = pl.BlockSpec(memory_space=pltpu.HBM)
CHIPS = ("y", "pair", "side")
PLANE = ("y", "run", "side")
PAIRS = [(0, 0), (0, 1), (1, 1), (0, 2), (1, 3), (2, 2), (2, 3), (3, 3), (2, 1), (3, 0)]


def call(kernel, shape, dtype, specs, scratch=()):
    return pl.pallas_call(
        kernel,
        out_shape=jax.ShapeDtypeStruct(shape, dtype),
        in_specs=specs,
        out_specs=VMEM,
        scratch_shapes=scratch,
        compiler_params=pltpu.CompilerParams(vmem_limit_bytes=32 * 1024 * 1024),
    )


def nn(a, b, precision=None):
    return lax.dot_general(
        a, b, (((1,), (0,)), ((), ())), precision=precision, preferred_element_type=jnp.float32
    )


def nt(a, b, precision=None):
    return lax.dot_general(
        a, b, (((1,), (1,)), ((), ())), precision=precision, preferred_element_type=jnp.float32
    )


def tn(a, b, precision=None):
    return lax.dot_general(
        a, b, (((0,), (0,)), ((), ())), precision=precision, preferred_element_type=jnp.float32
    )


def weigh_kernel(slab_hbm, chord_hbm, span_hbm, out_ref, slab_ref, chord_ref, span_ref, sems):
    copies = [
        pltpu.make_async_copy(slab_hbm, slab_ref, sems.at[0]),
        pltpu.make_async_copy(chord_hbm, chord_ref, sems.at[1]),
        pltpu.make_async_copy(span_hbm, span_ref, sems.at[2]),
    ]
    for copy in copies:
        copy.start()
    for copy in copies[::-1]:
        copy.wait()
    lane = lax.broadcasted_iota(jnp.int32, (1, LANES), 1)
    row = lax.broadcasted_iota(jnp.int32, (out_ref.shape[1], LANES), 0)
    chord = jnp.zeros(row.shape, jnp.float32)
    for i in range(out_ref.shape[1]):
        chord = jnp.where(row == i, chord_ref[i], chord)

    def weigh(tile):
        stations = jnp.where(lane < K, span_ref[2 * tile], span_ref[2 * tile + 1])
        block = slab_ref[0, :, tile * LANES : (tile + 1) * LANES].astype(jnp.float32)
        return block * chord * stations

    low_half = lane % K < K // 2
    for chip in range(out_ref.shape[0] // 2):
        first, second = weigh(2 * chip), weigh(2 * chip + 1)
        low = jnp.where(low_half, first, pltpu.roll(second, K // 2, 1))
        high = jnp.where(low_half, pltpu.roll(first, LANES - K // 2, 1), second)
        out_ref[2 * chip] = low.astype(jnp.bfloat16)
        out_ref[2 * chip + 1] = high.astype(jnp.bfloat16)


def gram_kernel(own_ref, other_ref, out_ref):
    first = lax.axis_index("core") == 0
    crossed = [(0, 2), (1, 3)]
    for at, (i, j) in enumerate([(0, 0), (0, 1), (1, 1), *crossed]):
        total = None
        for part in range(2):
            left = own_ref[part, i * 128 : (i + 1) * 128, :]
            if j < 2:
                right = own_ref[part, j * 128 : (j + 1) * 128, :]
            else:
                low, high = other_ref[part, :128, :], other_ref[part, 128:, :]
                right = jnp.where(first == (j == 2), low, high)
            term = nt(left, right)
            total = term if total is None else total + term
        out_ref[at * 128 : (at + 1) * 128, :] = total


def inverse_cholesky(small):
    n = small.shape[0]
    wide = (8, 2 * n)
    eye = lax.broadcasted_iota(jnp.int32, (n, n), 0) == lax.broadcasted_iota(jnp.int32, (n, n), 1)
    both = jnp.concatenate([small, eye.astype(jnp.float32)], axis=1)
    blocks = [both[8 * b : 8 * b + 8] for b in range(n // 8)]
    sub = lax.broadcasted_iota(jnp.int32, wide, 0)
    rows = []
    for own in range(n // 8):
        panel = [
            {
                b: jnp.broadcast_to(blocks[b][:, 8 * own + k : 8 * own + k + 1], wide)
                for b in range(own, n // 8)
            }
            for k in range(8)
        ]
        pivots = None
        for k in range(8):
            pivot = jnp.broadcast_to(panel[k][own][k : k + 1], wide)
            pivots = pivot if pivots is None else jnp.where(sub >= k, pivot, pivots)
            inverse = 1.0 / pivot
            row = jnp.broadcast_to(blocks[own][k : k + 1], wide) * inverse
            column = dict(panel[k])
            column[own] = jnp.where(sub > k, column[own], 0.0)
            for later in range(k + 1, 8):
                scale = jnp.broadcast_to(panel[later][own][k : k + 1], wide) * inverse
                for b in range(own, n // 8):
                    panel[later][b] = panel[later][b] - column[b] * scale
            for b in range(own, n // 8):
                blocks[b] = blocks[b] - column[b] * row
        rows.append(blocks[own][:, n:] * lax.rsqrt(pivots)[:, n:])
    return jnp.concatenate(rows, axis=0)


def order_kernel(start_ref, out_ref):
    chords = start_ref.shape[1]
    source = lax.broadcasted_iota(jnp.int32, (chords, chords), 0)
    target = lax.broadcasted_iota(jnp.int32, (chords, chords), 1)
    half = chords // 2
    wanted = target % half // 4 * 8 + target // half * 4 + target % 4
    order = (source == wanted).astype(jnp.bfloat16)
    rest = start_ref[...]
    start = jnp.zeros_like(rest)
    for _ in range(3):
        part = rest.astype(jnp.bfloat16)
        rest = rest - part.astype(jnp.float32)
        start = start + nn(part, order)
    out_ref[...] = start


def factor_kernel(own_ref, other_ref, start_ref, own_fibres_ref, other_fibres_ref, out_ref, gram_ref):
    core = lax.axis_index("core")
    for at, (i, j) in enumerate(PAIRS):
        rows = pl.ds(at % 5 * 128, 128)
        mine = core == at // 5
        block = jnp.where(mine, own_ref[rows, :], other_ref[rows, :])
        gram_ref[i * 128 : (i + 1) * 128, j * 128 : (j + 1) * 128] = block
        if i != j:
            gram_ref[j * 128 : (j + 1) * 128, i * 128 : (i + 1) * 128] = block.T
    product = nn(start_ref[...], gram_ref[...], HIGHEST)
    for iteration in range(ITERS):
        small = nt(product, product, HIGHEST)
        if iteration < ITERS - 1:
            product = nn(product, gram_ref[...], HIGHEST)
        product = nn(inverse_cholesky(small), product, HIGHEST)
    half = gram_ref.shape[0] // 2
    narrow = product.astype(jnp.bfloat16)
    own = jnp.where(core == 0, own_fibres_ref[0], own_fibres_ref[1])
    other = jnp.where(core == 0, other_fibres_ref[0], other_fibres_ref[1])
    low, high = jnp.where(core == 0, own, other), jnp.where(core == 0, other, own)
    ranked = nn(narrow[:, :half], low) + nn(narrow[:, half:], high)
    out_ref[...] = ranked.astype(jnp.bfloat16).astype(jnp.float32)


def unfold_kernel(parts_ref, out_ref):
    chips = parts_ref.shape[0]
    chip = lax.broadcasted_iota(jnp.int32, (chips, 4 * chips), 0)
    station = lax.broadcasted_iota(jnp.int32, (chips, 4 * chips), 1)
    parts = parts_ref[...].astype(jnp.bfloat16)
    out = None
    for at in range(4):
        place = (station == 4 * chip + at).astype(jnp.bfloat16)
        lane = K * (at % 2) + K // 2 * (at // 2)
        term = tn(parts[:, lane : lane + K // 2], place)
        out = term if out is None else out + term
    out_ref[0] = out.astype(jnp.bfloat16)


def swap(array, axes):
    return lax.all_to_all(array, axes, 0, 0, tiled=True)


def to_other_core(array):
    return lax.ppermute(array, "core", [(0, 1), (1, 0)])


def sum_everywhere(packed):
    shards = 32
    shard = (packed.shape[0] // shards // 4, 4, LANES)
    part = swap(packed.reshape(shards, *shard), PLANE).sum(0)
    part = swap(jnp.broadcast_to(part[None], (8, *shard)), "pair").sum(0)
    return swap(jnp.broadcast_to(part[None], (shards, *shard)), PLANE).reshape(packed.shape)


def per_device(slab, chord_weight, span_weight, start):
    rows, columns = slab.shape[1:]
    tiles = columns // LANES
    inputs = slab, chord_weight, span_weight
    scratch = [
        pltpu.VMEM(slab.shape, slab.dtype),
        pltpu.SMEM(chord_weight.shape, jnp.float32),
        pltpu.SMEM(span_weight.shape, jnp.float32),
        pltpu.SemaphoreType.DMA((3,)),
    ]
    send = call(weigh_kernel, (tiles, rows, LANES), jnp.bfloat16, [HBM] * 3, scratch)(
        *(pltpu.with_memory_space_constraint(array, pltpu.HBM) for array in inputs)
    )
    chips = tiles // 2
    received = swap(send.reshape(chips, 2, rows, LANES), CHIPS)
    own = received.transpose(1, 0, 2, 3).reshape(2, chips * rows, LANES)
    other = to_other_core(own)
    chords, rank = start.shape
    ordered = call(order_kernel, (rank, chords), jnp.float32, [VMEM])(start.T)
    half = call(gram_kernel, (len(PAIRS) // 2 * 128, 128), jnp.float32, [VMEM] * 2)(own, other)
    half = sum_everywhere(half)
    parts = call(
        factor_kernel,
        (rank, LANES),
        jnp.float32,
        [VMEM] * 5,
        [pltpu.VMEM((chords, chords), jnp.float32)],
    )(half, to_other_core(half), ordered, own, other)
    parts = swap(parts.reshape(rank, 1, LANES), CHIPS).reshape(rank, LANES)
    return call(unfold_kernel, (1, K // 2, 4 * rank), jnp.bfloat16, [VMEM])(parts)


def solution(mesh):
    fine = Mesh(mesh.devices.reshape(4, 8, 2, 2, 4), CHIPS + ("core", "run"))
    return jax.shard_map(
        per_device,
        mesh=fine,
        in_specs=(P("run", CHIPS + ("core",), None), P(CHIPS + ("core",)), P(), P()),
        out_specs=P("run", CHIPS + ("core",), None),
        check_vma=False,
    )
```

```python
import jax
import jax.numpy as jnp
from jax import lax
from jax.experimental import pallas as pl
from jax.experimental.pallas import tpu as pltpu
from jax.sharding import Mesh, PartitionSpec as P

K = 64
ITERS = 3
LANES = 128
WINDOW = 10
CHUNKS = 4
HIGHEST = lax.Precision.HIGHEST
VMEM = pl.BlockSpec(memory_space=pltpu.VMEM)
HBM = pl.BlockSpec(memory_space=pltpu.HBM)
CHIPS = ("y", "pair", "side")
PLANE = ("y", "run", "side")
PAIRS = [(0, 0), (0, 1), (1, 1), (0, 2), (1, 3), (2, 2), (2, 3), (3, 3), (2, 1), (3, 0)]


def call(kernel, shape, dtype, specs, scratch=()):
    return pl.pallas_call(
        kernel,
        out_shape=jax.ShapeDtypeStruct(shape, dtype),
        in_specs=specs,
        out_specs=VMEM,
        scratch_shapes=scratch,
        compiler_params=pltpu.CompilerParams(vmem_limit_bytes=32 * 1024 * 1024),
    )


def nn(a, b, precision=None):
    return lax.dot_general(
        a, b, (((1,), (0,)), ((), ())), precision=precision, preferred_element_type=jnp.float32
    )


def nt(a, b, precision=None):
    return lax.dot_general(
        a, b, (((1,), (1,)), ((), ())), precision=precision, preferred_element_type=jnp.float32
    )


def tn(a, b, precision=None):
    return lax.dot_general(
        a, b, (((0,), (0,)), ((), ())), precision=precision, preferred_element_type=jnp.float32
    )


def weigh_kernel(slab_hbm, chord_hbm, span_hbm, out_ref, slab_ref, chord_ref, span_ref, sems):
    weights = [
        pltpu.make_async_copy(chord_hbm, chord_ref, sems.at[0]),
        pltpu.make_async_copy(span_hbm, span_ref, sems.at[1]),
    ]
    width = slab_ref.shape[2] // CHUNKS
    chunks = []
    for at in range(CHUNKS):
        part = pl.ds(at * width, width)
        chunks.append(
            pltpu.make_async_copy(
                slab_hbm.at[:, :, part], slab_ref.at[:, :, part], sems.at[2 + at]
            )
        )
    for copy in weights + chunks:
        copy.start()
    for copy in weights:
        copy.wait()
    lane = lax.broadcasted_iota(jnp.int32, (1, LANES), 1)
    row = lax.broadcasted_iota(jnp.int32, (out_ref.shape[1], LANES), 0)
    chord = jnp.zeros(row.shape, jnp.float32)
    for i in range(out_ref.shape[1]):
        chord = jnp.where(row == i, chord_ref[i], chord)

    def weigh(tile):
        stations = jnp.where(lane < K, span_ref[2 * tile], span_ref[2 * tile + 1])
        block = slab_ref[0, :, tile * LANES : (tile + 1) * LANES].astype(jnp.float32)
        return block * chord * stations

    low_half = lane % K < K // 2
    chips = out_ref.shape[0] // 2
    for chip in range(chips):
        if chip % (chips // CHUNKS) == 0:
            chunks[chip // (chips // CHUNKS)].wait()
        first, second = weigh(2 * chip), weigh(2 * chip + 1)
        low = jnp.where(low_half, first, pltpu.roll(second, K // 2, 1))
        high = jnp.where(low_half, pltpu.roll(first, LANES - K // 2, 1), second)
        out_ref[2 * chip] = low.astype(jnp.bfloat16)
        out_ref[2 * chip + 1] = high.astype(jnp.bfloat16)


def gram_kernel(own_ref, other_ref, out_ref):
    first = lax.axis_index("core") == 0
    crossed = [(0, 2), (1, 3)]
    for at, (i, j) in enumerate([(0, 0), (0, 1), (1, 1), *crossed]):
        total = None
        for part in range(2):
            left = own_ref[part, i * 128 : (i + 1) * 128, :]
            if j < 2:
                right = own_ref[part, j * 128 : (j + 1) * 128, :]
            else:
                low, high = other_ref[part, :128, :], other_ref[part, 128:, :]
                right = jnp.where(first == (j == 2), low, high)
            term = nt(left, right)
            total = term if total is None else total + term
        out_ref[at * 128 : (at + 1) * 128, :] = total


def inverse_cholesky(small):
    n = small.shape[0]
    wide = (8, 2 * n)
    eye = lax.broadcasted_iota(jnp.int32, (n, n), 0) == lax.broadcasted_iota(jnp.int32, (n, n), 1)
    both = jnp.concatenate([small, eye.astype(jnp.float32)], axis=1)
    blocks = [both[8 * b : 8 * b + 8] for b in range(n // 8)]
    sub = lax.broadcasted_iota(jnp.int32, wide, 0)

    def spread(column, since):
        return {
            b: jnp.broadcast_to(blocks[b][:, column : column + 1], wide)
            for b in range(since, n // 8)
        }

    ahead = {column: spread(column, 0) for column in range(WINDOW)}
    pivots = [None] * (n // 8)
    for j in range(n):
        own, k = divmod(j, 8)
        column = ahead.pop(j)
        pivot = jnp.broadcast_to(column[own][k : k + 1], wide)
        pivots[own] = pivot if k == 0 else jnp.where(sub >= k, pivot, pivots[own])
        inverse = 1.0 / pivot
        row = jnp.broadcast_to(blocks[own][k : k + 1], wide) * inverse
        column[own] = jnp.where(sub > k, column[own], 0.0)
        for later in ahead.values():
            scale = jnp.broadcast_to(later[own][k : k + 1], wide) * inverse
            for b in range(own, n // 8):
                later[b] = later[b] - column[b] * scale
        for b in range(own, n // 8):
            blocks[b] = blocks[b] - column[b] * row
        if j + WINDOW < n:
            ahead[j + WINDOW] = spread(j + WINDOW, (j + 1) // 8)
    rows = [block[:, n:] * lax.rsqrt(p)[:, n:] for block, p in zip(blocks, pivots)]
    return jnp.concatenate(rows, axis=0)


def order_kernel(start_ref, out_ref):
    chords = start_ref.shape[1]
    source = lax.broadcasted_iota(jnp.int32, (chords, chords), 0)
    target = lax.broadcasted_iota(jnp.int32, (chords, chords), 1)
    half = chords // 2
    wanted = target % half // 4 * 8 + target // half * 4 + target % 4
    order = (source == wanted).astype(jnp.bfloat16)
    rest = start_ref[...]
    start = jnp.zeros_like(rest)
    for _ in range(3):
        part = rest.astype(jnp.bfloat16)
        rest = rest - part.astype(jnp.float32)
        start = start + nn(part, order)
    out_ref[...] = start


def factor_kernel(own_ref, other_ref, start_ref, own_fibres_ref, other_fibres_ref, out_ref, gram_ref):
    core = lax.axis_index("core")
    for at, (i, j) in enumerate(PAIRS):
        rows = pl.ds(at % 5 * 128, 128)
        mine = core == at // 5
        block = jnp.where(mine, own_ref[rows, :], other_ref[rows, :])
        gram_ref[i * 128 : (i + 1) * 128, j * 128 : (j + 1) * 128] = block
        if i != j:
            gram_ref[j * 128 : (j + 1) * 128, i * 128 : (i + 1) * 128] = block.T
    product = nn(start_ref[...], gram_ref[...], HIGHEST)
    for iteration in range(ITERS):
        small = nt(product, product, HIGHEST)
        if iteration < ITERS - 1:
            product = nn(product, gram_ref[...], HIGHEST)
        product = nn(inverse_cholesky(small), product, HIGHEST)
    half = gram_ref.shape[0] // 2
    narrow = product.astype(jnp.bfloat16)
    own = jnp.where(core == 0, own_fibres_ref[0], own_fibres_ref[1])
    other = jnp.where(core == 0, other_fibres_ref[0], other_fibres_ref[1])
    low, high = jnp.where(core == 0, own, other), jnp.where(core == 0, other, own)
    ranked = nn(narrow[:, :half], low) + nn(narrow[:, half:], high)
    out_ref[...] = ranked.astype(jnp.bfloat16).astype(jnp.float32)


def unfold_kernel(parts_ref, out_ref):
    chips = parts_ref.shape[0]
    chip = lax.broadcasted_iota(jnp.int32, (chips, 4 * chips), 0)
    station = lax.broadcasted_iota(jnp.int32, (chips, 4 * chips), 1)
    parts = parts_ref[...].astype(jnp.bfloat16)
    out = None
    for at in range(4):
        place = (station == 4 * chip + at).astype(jnp.bfloat16)
        lane = K * (at % 2) + K // 2 * (at // 2)
        term = tn(parts[:, lane : lane + K // 2], place)
        out = term if out is None else out + term
    out_ref[0] = out.astype(jnp.bfloat16)


def swap(array, axes):
    return lax.all_to_all(array, axes, 0, 0, tiled=True)


def to_other_core(array):
    return lax.ppermute(array, "core", [(0, 1), (1, 0)])


def sum_everywhere(packed):
    shards = 32
    shard = (packed.shape[0] // shards // 4, 4, LANES)
    part = swap(packed.reshape(shards, *shard), PLANE).sum(0)
    part = swap(jnp.broadcast_to(part[None], (8, *shard)), "pair").sum(0)
    return swap(jnp.broadcast_to(part[None], (shards, *shard)), PLANE).reshape(packed.shape)


def per_device(slab, chord_weight, span_weight, start):
    rows, columns = slab.shape[1:]
    tiles = columns // LANES
    inputs = slab, chord_weight, span_weight
    scratch = [
        pltpu.VMEM(slab.shape, slab.dtype),
        pltpu.SMEM(chord_weight.shape, jnp.float32),
        pltpu.SMEM(span_weight.shape, jnp.float32),
        pltpu.SemaphoreType.DMA((2 + CHUNKS,)),
    ]
    send = call(weigh_kernel, (tiles, rows, LANES), jnp.bfloat16, [HBM] * 3, scratch)(
        *(pltpu.with_memory_space_constraint(array, pltpu.HBM) for array in inputs)
    )
    chips = tiles // 2
    received = swap(send.reshape(chips, 2, rows, LANES), CHIPS)
    own = received.transpose(1, 0, 2, 3).reshape(2, chips * rows, LANES)
    other = to_other_core(own)
    chords, rank = start.shape
    ordered = call(order_kernel, (rank, chords), jnp.float32, [VMEM])(start.T)
    half = call(gram_kernel, (len(PAIRS) // 2 * 128, 128), jnp.float32, [VMEM] * 2)(own, other)
    half = sum_everywhere(half)
    parts = call(
        factor_kernel,
        (rank, LANES),
        jnp.float32,
        [VMEM] * 5,
        [pltpu.VMEM((chords, chords), jnp.float32)],
    )(half, to_other_core(half), ordered, own, other)
    parts = swap(parts.reshape(rank, 1, LANES), CHIPS).reshape(rank, LANES)
    return call(unfold_kernel, (1, K // 2, 4 * rank), jnp.bfloat16, [VMEM])(parts)


def solution(mesh):
    fine = Mesh(mesh.devices.reshape(4, 8, 2, 2, 4), CHIPS + ("core", "run"))
    return jax.shard_map(
        per_device,
        mesh=fine,
        in_specs=(P("run", CHIPS + ("core",), None), P(CHIPS + ("core",)), P(), P()),
        out_specs=P("run", CHIPS + ("core",), None),
        check_vma=False,
    )
```

```python
import jax
import jax.numpy as jnp
from jax import lax
from jax.experimental import pallas as pl
from jax.experimental.pallas import tpu as pltpu
from jax.sharding import Mesh, PartitionSpec as P

K = 64
ITERS = 3
LANES = 128
WINDOW = 10
HIGHEST = lax.Precision.HIGHEST
VMEM = pl.BlockSpec(memory_space=pltpu.VMEM)
HBM = pl.BlockSpec(memory_space=pltpu.HBM)
CHIPS = ("y", "pair", "side")
PLANE = ("y", "run", "side")
PAIRS = [(0, 0), (0, 1), (1, 1), (0, 2), (1, 3), (2, 2), (2, 3), (3, 3), (2, 1), (3, 0)]


def call(kernel, shape, dtype, specs, scratch=()):
    return pl.pallas_call(
        kernel,
        out_shape=jax.ShapeDtypeStruct(shape, dtype),
        in_specs=specs,
        out_specs=VMEM,
        scratch_shapes=scratch,
        compiler_params=pltpu.CompilerParams(vmem_limit_bytes=32 * 1024 * 1024),
    )


def nn(a, b, precision=None):
    return lax.dot_general(
        a, b, (((1,), (0,)), ((), ())), precision=precision, preferred_element_type=jnp.float32
    )


def nt(a, b, precision=None):
    return lax.dot_general(
        a, b, (((1,), (1,)), ((), ())), precision=precision, preferred_element_type=jnp.float32
    )


def tn(a, b, precision=None):
    return lax.dot_general(
        a, b, (((0,), (0,)), ((), ())), precision=precision, preferred_element_type=jnp.float32
    )


def weigh_kernel(slab_hbm, chord_hbm, span_hbm, out_ref, slab_ref, chord_ref, span_ref, sems):
    copies = [
        pltpu.make_async_copy(slab_hbm, slab_ref, sems.at[0]),
        pltpu.make_async_copy(chord_hbm, chord_ref, sems.at[1]),
        pltpu.make_async_copy(span_hbm, span_ref, sems.at[2]),
    ]
    for copy in copies:
        copy.start()
    for copy in copies[::-1]:
        copy.wait()
    lane = lax.broadcasted_iota(jnp.int32, (1, LANES), 1)
    row = lax.broadcasted_iota(jnp.int32, (out_ref.shape[1], LANES), 0)
    chord = jnp.zeros(row.shape, jnp.float32)
    for i in range(out_ref.shape[1]):
        chord = jnp.where(row == i, chord_ref[i], chord)

    def weigh(tile):
        stations = jnp.where(lane < K, span_ref[2 * tile], span_ref[2 * tile + 1])
        block = slab_ref[0, :, tile * LANES : (tile + 1) * LANES].astype(jnp.float32)
        return block * chord * stations

    low_half = lane % K < K // 2
    for chip in range(out_ref.shape[0] // 2):
        first, second = weigh(2 * chip), weigh(2 * chip + 1)
        low = jnp.where(low_half, first, pltpu.roll(second, K // 2, 1))
        high = jnp.where(low_half, pltpu.roll(first, LANES - K // 2, 1), second)
        out_ref[2 * chip] = low.astype(jnp.bfloat16)
        out_ref[2 * chip + 1] = high.astype(jnp.bfloat16)


def gram_kernel(own_ref, other_ref, out_ref):
    first = lax.axis_index("core") == 0
    crossed = [(0, 2), (1, 3)]
    for at, (i, j) in enumerate([(0, 0), (0, 1), (1, 1), *crossed]):
        total = None
        for part in range(2):
            left = own_ref[part, i * 128 : (i + 1) * 128, :]
            if j < 2:
                right = own_ref[part, j * 128 : (j + 1) * 128, :]
            else:
                low, high = other_ref[part, :128, :], other_ref[part, 128:, :]
                right = jnp.where(first == (j == 2), low, high)
            term = nt(left, right)
            total = term if total is None else total + term
        out_ref[at * 128 : (at + 1) * 128, :] = total


def inverse_cholesky(small):
    n = small.shape[0]
    wide = (8, 2 * n)
    eye = lax.broadcasted_iota(jnp.int32, (n, n), 0) == lax.broadcasted_iota(jnp.int32, (n, n), 1)
    both = jnp.concatenate([small, eye.astype(jnp.float32)], axis=1)
    blocks = [both[8 * b : 8 * b + 8] for b in range(n // 8)]
    sub = lax.broadcasted_iota(jnp.int32, wide, 0)

    def spread(column, since):
        return {
            b: jnp.broadcast_to(blocks[b][:, column : column + 1], wide)
            for b in range(since, n // 8)
        }

    ahead = {column: spread(column, 0) for column in range(WINDOW)}
    pivots = [None] * (n // 8)
    for j in range(n):
        own, k = divmod(j, 8)
        column = ahead.pop(j)
        pivot = jnp.broadcast_to(column[own][k : k + 1], wide)
        pivots[own] = pivot if k == 0 else jnp.where(sub >= k, pivot, pivots[own])
        inverse = 1.0 / pivot
        row = jnp.broadcast_to(blocks[own][k : k + 1], wide) * inverse
        column[own] = jnp.where(sub > k, column[own], 0.0)
        for later in ahead.values():
            scale = jnp.broadcast_to(later[own][k : k + 1], wide) * inverse
            for b in range(own, n // 8):
                later[b] = later[b] - column[b] * scale
        for b in range(own, n // 8):
            blocks[b] = blocks[b] - column[b] * row
        if j + WINDOW < n:
            ahead[j + WINDOW] = spread(j + WINDOW, (j + 1) // 8)
    rows = [block[:, n:] * lax.rsqrt(p)[:, n:] for block, p in zip(blocks, pivots)]
    return jnp.concatenate(rows, axis=0)


def order_kernel(start_ref, out_ref):
    chords = start_ref.shape[1]
    source = lax.broadcasted_iota(jnp.int32, (chords, chords), 0)
    target = lax.broadcasted_iota(jnp.int32, (chords, chords), 1)
    half = chords // 2
    wanted = target % half // 4 * 8 + target // half * 4 + target % 4
    order = (source == wanted).astype(jnp.bfloat16)
    rest = start_ref[...]
    start = jnp.zeros_like(rest)
    for _ in range(3):
        part = rest.astype(jnp.bfloat16)
        rest = rest - part.astype(jnp.float32)
        start = start + nn(part, order)
    out_ref[...] = start


def factor_kernel(packed_ref, start_ref, own_fibres_ref, other_fibres_ref, out_ref, gram_ref):
    core = lax.axis_index("core")
    for at, (i, j) in enumerate(PAIRS):
        block = packed_ref[at * 128 : (at + 1) * 128, :]
        gram_ref[i * 128 : (i + 1) * 128, j * 128 : (j + 1) * 128] = block
        if i != j:
            gram_ref[j * 128 : (j + 1) * 128, i * 128 : (i + 1) * 128] = block.T
    product = nn(start_ref[...], gram_ref[...], HIGHEST)
    for iteration in range(ITERS):
        small = nt(product, product, HIGHEST)
        if iteration < ITERS - 1:
            product = nn(product, gram_ref[...], HIGHEST)
        product = nn(inverse_cholesky(small), product, HIGHEST)
    half = gram_ref.shape[0] // 2
    narrow = product.astype(jnp.bfloat16)
    own = jnp.where(core == 0, own_fibres_ref[0], own_fibres_ref[1])
    other = jnp.where(core == 0, other_fibres_ref[0], other_fibres_ref[1])
    low, high = jnp.where(core == 0, own, other), jnp.where(core == 0, other, own)
    ranked = nn(narrow[:, :half], low) + nn(narrow[:, half:], high)
    out_ref[...] = ranked.astype(jnp.bfloat16).astype(jnp.float32)


def unfold_kernel(parts_ref, out_ref):
    chips = parts_ref.shape[0]
    chip = lax.broadcasted_iota(jnp.int32, (chips, 4 * chips), 0)
    station = lax.broadcasted_iota(jnp.int32, (chips, 4 * chips), 1)
    parts = parts_ref[...].astype(jnp.bfloat16)
    out = None
    for at in range(4):
        place = (station == 4 * chip + at).astype(jnp.bfloat16)
        lane = K * (at % 2) + K // 2 * (at // 2)
        term = tn(parts[:, lane : lane + K // 2], place)
        out = term if out is None else out + term
    out_ref[0] = out.astype(jnp.bfloat16)


def swap(array, axes):
    return lax.all_to_all(array, axes, 0, 0, tiled=True)


def to_other_core(array):
    return lax.ppermute(array, "core", [(0, 1), (1, 0)])


def sum_everywhere(half):
    shards = 32
    shard = (half.shape[0] // shards // 4, 4, LANES)
    part = swap(half.reshape(shards, *shard), PLANE).sum(0)
    part = swap(jnp.broadcast_to(part[None], (8, *shard)), "pair").sum(0)
    part = jnp.broadcast_to(part[None], (2 * shards, *shard))
    return swap(part, ("core", *PLANE)).reshape(2 * half.shape[0], LANES)


def per_device(slab, chord_weight, span_weight, start):
    rows, columns = slab.shape[1:]
    tiles = columns // LANES
    inputs = slab, chord_weight, span_weight
    scratch = [
        pltpu.VMEM(slab.shape, slab.dtype),
        pltpu.SMEM(chord_weight.shape, jnp.float32),
        pltpu.SMEM(span_weight.shape, jnp.float32),
        pltpu.SemaphoreType.DMA((3,)),
    ]
    send = call(weigh_kernel, (tiles, rows, LANES), jnp.bfloat16, [HBM] * 3, scratch)(
        *(pltpu.with_memory_space_constraint(array, pltpu.HBM) for array in inputs)
    )
    chips = tiles // 2
    received = swap(send.reshape(chips, 2, rows, LANES), CHIPS)
    own = received.transpose(1, 0, 2, 3).reshape(2, chips * rows, LANES)
    other = to_other_core(own)
    chords, rank = start.shape
    ordered = call(order_kernel, (rank, chords), jnp.float32, [VMEM])(start.T)
    half = call(gram_kernel, (len(PAIRS) // 2 * 128, 128), jnp.float32, [VMEM] * 2)(own, other)
    packed = sum_everywhere(half)
    parts = call(
        factor_kernel,
        (rank, LANES),
        jnp.float32,
        [VMEM] * 4,
        [pltpu.VMEM((chords, chords), jnp.float32)],
    )(packed, ordered, own, other)
    parts = swap(parts.reshape(rank, 1, LANES), CHIPS).reshape(rank, LANES)
    return call(unfold_kernel, (1, K // 2, 4 * rank), jnp.bfloat16, [VMEM])(parts)


def solution(mesh):
    fine = Mesh(mesh.devices.reshape(4, 8, 2, 2, 4), CHIPS + ("core", "run"))
    return jax.shard_map(
        per_device,
        mesh=fine,
        in_specs=(P("run", CHIPS + ("core",), None), P(CHIPS + ("core",)), P(), P()),
        out_specs=P("run", CHIPS + ("core",), None),
        check_vma=False,
    )
```

```python
import jax
import jax.numpy as jnp
from jax import lax
from jax.experimental import pallas as pl
from jax.experimental.pallas import tpu as pltpu
from jax.sharding import Mesh, PartitionSpec as P

K = 64
ITERS = 3
LANES = 128
WINDOW = 10
HIGHEST = lax.Precision.HIGHEST
VMEM = pl.BlockSpec(memory_space=pltpu.VMEM)
HBM = pl.BlockSpec(memory_space=pltpu.HBM)
CHIPS = ("y", "pair", "side")
PLANE = ("y", "run", "side")
PAIRS = [(i, j) for i in range(4) for j in range(i, 4)]


def call(kernel, shape, dtype, specs, scratch=()):
    return pl.pallas_call(
        kernel,
        out_shape=jax.ShapeDtypeStruct(shape, dtype),
        in_specs=specs,
        out_specs=VMEM,
        scratch_shapes=scratch,
        compiler_params=pltpu.CompilerParams(vmem_limit_bytes=32 * 1024 * 1024),
    )


def nn(a, b, precision=None):
    return lax.dot_general(
        a, b, (((1,), (0,)), ((), ())), precision=precision, preferred_element_type=jnp.float32
    )


def nt(a, b, precision=None):
    return lax.dot_general(
        a, b, (((1,), (1,)), ((), ())), precision=precision, preferred_element_type=jnp.float32
    )


def tn(a, b, precision=None):
    return lax.dot_general(
        a, b, (((0,), (0,)), ((), ())), precision=precision, preferred_element_type=jnp.float32
    )


def weigh_kernel(slab_hbm, chord_hbm, span_hbm, out_ref, slab_ref, chord_ref, span_ref, sems):
    copies = [
        pltpu.make_async_copy(slab_hbm, slab_ref, sems.at[0]),
        pltpu.make_async_copy(chord_hbm, chord_ref, sems.at[1]),
        pltpu.make_async_copy(span_hbm, span_ref, sems.at[2]),
    ]
    for copy in copies:
        copy.start()
    for copy in copies[::-1]:
        copy.wait()
    lane = lax.broadcasted_iota(jnp.int32, (1, LANES), 1)
    row = lax.broadcasted_iota(jnp.int32, (out_ref.shape[1], LANES), 0)
    chord = jnp.zeros(row.shape, jnp.float32)
    for i in range(out_ref.shape[1]):
        chord = jnp.where(row == i, chord_ref[i], chord)

    def weigh(tile):
        stations = jnp.where(lane < K, span_ref[2 * tile], span_ref[2 * tile + 1])
        block = slab_ref[0, :, tile * LANES : (tile + 1) * LANES].astype(jnp.float32)
        return block * chord * stations

    low_half = lane % K < K // 2
    for chip in range(out_ref.shape[0] // 2):
        first, second = weigh(2 * chip), weigh(2 * chip + 1)
        low = jnp.where(low_half, first, pltpu.roll(second, K // 2, 1))
        high = jnp.where(low_half, pltpu.roll(first, LANES - K // 2, 1), second)
        out_ref[2 * chip] = low.astype(jnp.bfloat16)
        out_ref[2 * chip + 1] = high.astype(jnp.bfloat16)


def gram_kernel(fibres_ref, out_ref):
    core = lax.axis_index("core")
    count = len(PAIRS) // 2

    def make(pairs):
        for at, (i, j) in enumerate(pairs):
            left, right = pl.ds(i * 128, 128), pl.ds(j * 128, 128)
            out_ref[at * 128 : (at + 1) * 128, :] = nt(
                fibres_ref[0, left, :], fibres_ref[0, right, :]
            ) + nt(fibres_ref[1, left, :], fibres_ref[1, right, :])

    @pl.when(core == 0)
    def _():
        make(PAIRS[:count])

    @pl.when(core != 0)
    def _():
        make(PAIRS[count:])


def inverse_cholesky(small):
    n = small.shape[0]
    wide = (8, 2 * n)
    eye = lax.broadcasted_iota(jnp.int32, (n, n), 0) == lax.broadcasted_iota(jnp.int32, (n, n), 1)
    both = jnp.concatenate([small, eye.astype(jnp.float32)], axis=1)
    blocks = [both[8 * b : 8 * b + 8] for b in range(n // 8)]
    sub = lax.broadcasted_iota(jnp.int32, wide, 0)

    def spread(column, since):
        return {
            b: jnp.broadcast_to(blocks[b][:, column : column + 1], wide)
            for b in range(since, n // 8)
        }

    ahead = {column: spread(column, 0) for column in range(WINDOW)}
    pivots = [None] * (n // 8)
    for j in range(n):
        own, k = divmod(j, 8)
        column = ahead.pop(j)
        pivot = jnp.broadcast_to(column[own][k : k + 1], wide)
        pivots[own] = pivot if k == 0 else jnp.where(sub >= k, pivot, pivots[own])
        inverse = 1.0 / pivot
        row = jnp.broadcast_to(blocks[own][k : k + 1], wide) * inverse
        column[own] = jnp.where(sub > k, column[own], 0.0)
        for later in ahead.values():
            scale = jnp.broadcast_to(later[own][k : k + 1], wide) * inverse
            for b in range(own, n // 8):
                later[b] = later[b] - column[b] * scale
        for b in range(own, n // 8):
            blocks[b] = blocks[b] - column[b] * row
        if j + WINDOW < n:
            ahead[j + WINDOW] = spread(j + WINDOW, (j + 1) // 8)
    rows = [block[:, n:] * lax.rsqrt(p)[:, n:] for block, p in zip(blocks, pivots)]
    return jnp.concatenate(rows, axis=0)


def factor_kernel(packed_ref, start_ref, fibres_ref, out_ref, gram_ref):
    for at, (i, j) in enumerate(PAIRS):
        block = packed_ref[at * 128 : (at + 1) * 128, :]
        gram_ref[i * 128 : (i + 1) * 128, j * 128 : (j + 1) * 128] = block
        if i != j:
            gram_ref[j * 128 : (j + 1) * 128, i * 128 : (i + 1) * 128] = block.T
    product = nn(start_ref[...], gram_ref[...], HIGHEST)
    for iteration in range(ITERS):
        small = nt(product, product, HIGHEST)
        if iteration < ITERS - 1:
            product = nn(product, gram_ref[...], HIGHEST)
        product = nn(inverse_cholesky(small), product, HIGHEST)
    core = lax.axis_index("core")
    fibres = jnp.where(core == 0, fibres_ref[0], fibres_ref[1])
    ranked = nn(product.astype(jnp.bfloat16), fibres)
    out_ref[...] = ranked.astype(jnp.bfloat16).astype(jnp.float32)


def unfold_kernel(parts_ref, out_ref):
    chips = parts_ref.shape[0]
    chip = lax.broadcasted_iota(jnp.int32, (chips, 4 * chips), 0)
    station = lax.broadcasted_iota(jnp.int32, (chips, 4 * chips), 1)
    parts = parts_ref[...].astype(jnp.bfloat16)
    out = None
    for at in range(4):
        place = (station == 4 * chip + at).astype(jnp.bfloat16)
        lane = K * (at % 2) + K // 2 * (at // 2)
        term = tn(parts[:, lane : lane + K // 2], place)
        out = term if out is None else out + term
    out_ref[0] = out.astype(jnp.bfloat16)


def swap(array, axes):
    return lax.all_to_all(array, axes, 0, 0, tiled=True)


def from_both_cores(array):
    return lax.all_gather(array, "core", axis=0)


def sum_everywhere(packed):
    shards = 32
    shard = (packed.shape[0] // shards // 4, 4, LANES)
    part = swap(packed.reshape(shards, *shard), PLANE).sum(0)
    part = swap(jnp.broadcast_to(part[None], (8, *shard)), "pair").sum(0)
    return swap(jnp.broadcast_to(part[None], (shards, *shard)), PLANE).reshape(packed.shape)


def per_device(slab, chord_weight, span_weight, start):
    rows, columns = slab.shape[1:]
    tiles = columns // LANES
    inputs = slab, chord_weight, span_weight
    scratch = [
        pltpu.VMEM(slab.shape, slab.dtype),
        pltpu.SMEM(chord_weight.shape, jnp.float32),
        pltpu.SMEM(span_weight.shape, jnp.float32),
        pltpu.SemaphoreType.DMA((3,)),
    ]
    send = call(weigh_kernel, (tiles, rows, LANES), jnp.bfloat16, [HBM] * 3, scratch)(
        *(pltpu.with_memory_space_constraint(array, pltpu.HBM) for array in inputs)
    )
    chips = tiles // 2
    received = swap(send.reshape(chips, 2, rows, LANES), CHIPS)
    received = from_both_cores(received.reshape(tiles * rows, LANES))
    fibres = lax.optimization_barrier(received).reshape(2, chips, 2, rows, LANES)
    fibres = fibres.transpose(2, 1, 0, 3, 4).reshape(2, tiles * rows, LANES)
    half = call(gram_kernel, (len(PAIRS) // 2 * 128, 128), jnp.float32, [VMEM])(fibres)
    packed = from_both_cores(sum_everywhere(half)).reshape(len(PAIRS) * 128, 128)
    chords, rank = start.shape
    parts = call(
        factor_kernel,
        (rank, LANES),
        jnp.float32,
        [VMEM] * 3,
        [pltpu.VMEM((chords, chords), jnp.float32)],
    )(packed, start.T, fibres)
    parts = swap(parts.reshape(rank, 1, LANES), CHIPS).reshape(rank, LANES)
    return call(unfold_kernel, (1, K // 2, 4 * rank), jnp.bfloat16, [VMEM])(parts)


def solution(mesh):
    fine = Mesh(mesh.devices.reshape(4, 8, 2, 2, 4), CHIPS + ("core", "run"))
    return jax.shard_map(
        per_device,
        mesh=fine,
        in_specs=(P("run", CHIPS + ("core",), None), P(CHIPS + ("core",)), P(), P()),
        out_specs=P("run", CHIPS + ("core",), None),
        check_vma=False,
    )
```

```python
import jax
import jax.numpy as jnp
from jax import lax
from jax.experimental import pallas as pl
from jax.experimental.pallas import tpu as pltpu
from jax.sharding import Mesh, PartitionSpec as P

K = 64
ITERS = 3
LANES = 128
WINDOW = 10
HIGHEST = lax.Precision.HIGHEST
VMEM = pl.BlockSpec(memory_space=pltpu.VMEM)
HBM = pl.BlockSpec(memory_space=pltpu.HBM)
CHIPS = ("y", "pair", "side")
PLANE = ("y", "run", "side")
SHARES = [((0, 1), [(0, 1), (0, 2), (0, 3)]), ((2, 3), [(1, 2), (1, 3), (2, 3)])]
SHARE_ROWS = 576


def call(kernel, shape, dtype, specs, scratch=()):
    return pl.pallas_call(
        kernel,
        out_shape=jax.ShapeDtypeStruct(shape, dtype),
        in_specs=specs,
        out_specs=VMEM,
        scratch_shapes=scratch,
        compiler_params=pltpu.CompilerParams(vmem_limit_bytes=32 * 1024 * 1024),
    )


def nn(a, b, precision=None):
    return lax.dot_general(
        a, b, (((1,), (0,)), ((), ())), precision=precision, preferred_element_type=jnp.float32
    )


def nt(a, b, precision=None):
    return lax.dot_general(
        a, b, (((1,), (1,)), ((), ())), precision=precision, preferred_element_type=jnp.float32
    )


def tn(a, b, precision=None):
    return lax.dot_general(
        a, b, (((0,), (0,)), ((), ())), precision=precision, preferred_element_type=jnp.float32
    )


def weigh_kernel(slab_hbm, chord_hbm, span_hbm, out_ref, slab_ref, chord_ref, span_ref, sems):
    copies = [
        pltpu.make_async_copy(slab_hbm, slab_ref, sems.at[0]),
        pltpu.make_async_copy(chord_hbm, chord_ref, sems.at[1]),
        pltpu.make_async_copy(span_hbm, span_ref, sems.at[2]),
    ]
    for copy in copies:
        copy.start()
    for copy in copies[::-1]:
        copy.wait()
    lane = lax.broadcasted_iota(jnp.int32, (1, LANES), 1)
    row = lax.broadcasted_iota(jnp.int32, (out_ref.shape[1], LANES), 0)
    chord = jnp.zeros(row.shape, jnp.float32)
    for i in range(out_ref.shape[1]):
        chord = jnp.where(row == i, chord_ref[i], chord)

    def weigh(tile):
        stations = jnp.where(lane < K, span_ref[2 * tile], span_ref[2 * tile + 1])
        block = slab_ref[0, :, tile * LANES : (tile + 1) * LANES].astype(jnp.float32)
        return block * chord * stations

    low_half = lane % K < K // 2
    for chip in range(out_ref.shape[0] // 2):
        first, second = weigh(2 * chip), weigh(2 * chip + 1)
        low = jnp.where(low_half, first, pltpu.roll(second, K // 2, 1))
        high = jnp.where(low_half, pltpu.roll(first, LANES - K // 2, 1), second)
        out_ref[2 * chip] = low.astype(jnp.bfloat16)
        out_ref[2 * chip + 1] = high.astype(jnp.bfloat16)


def square_indices():
    return (lax.broadcasted_iota(jnp.int32, (128, 128), axis) for axis in range(2))


def gram_kernel(fibres_ref, out_ref):
    core = lax.axis_index("core")

    def block(i, j):
        left, right = pl.ds(i * 128, 128), pl.ds(j * 128, 128)
        return nt(fibres_ref[0, left, :], fibres_ref[0, right, :]) + nt(
            fibres_ref[1, left, :], fibres_ref[1, right, :]
        )

    def make(diagonal, pairs):
        row, column = square_indices()
        first, second = (block(i, i) for i in diagonal)
        out_ref[:128, :] = jnp.where(row <= column, first, second)
        for at, (i, j) in enumerate(pairs, 1):
            out_ref[at * 128 : (at + 1) * 128, :] = block(i, j)
        rest = jnp.sum(jnp.where(row == column, second, 0.0), axis=0, keepdims=True)
        row = row[: SHARE_ROWS - 512]
        out_ref[512:, :] = jnp.where(row == 0, rest, 0.0)

    for own, share in enumerate(SHARES):
        pl.when(core == own)(lambda share=share: make(*share))


def inverse_cholesky(small):
    n = small.shape[0]
    wide = (8, 2 * n)
    eye = lax.broadcasted_iota(jnp.int32, (n, n), 0) == lax.broadcasted_iota(jnp.int32, (n, n), 1)
    both = jnp.concatenate([small, eye.astype(jnp.float32)], axis=1)
    blocks = [both[8 * b : 8 * b + 8] for b in range(n // 8)]
    sub = lax.broadcasted_iota(jnp.int32, wide, 0)

    def spread(column, since):
        return {
            b: jnp.broadcast_to(blocks[b][:, column : column + 1], wide)
            for b in range(since, n // 8)
        }

    ahead = {column: spread(column, 0) for column in range(WINDOW)}
    pivots = [None] * (n // 8)
    for j in range(n):
        own, k = divmod(j, 8)
        column = ahead.pop(j)
        pivot = jnp.broadcast_to(column[own][k : k + 1], wide)
        pivots[own] = pivot if k == 0 else jnp.where(sub >= k, pivot, pivots[own])
        inverse = 1.0 / pivot
        row = jnp.broadcast_to(blocks[own][k : k + 1], wide) * inverse
        column[own] = jnp.where(sub > k, column[own], 0.0)
        for later in ahead.values():
            scale = jnp.broadcast_to(later[own][k : k + 1], wide) * inverse
            for b in range(own, n // 8):
                later[b] = later[b] - column[b] * scale
        for b in range(own, n // 8):
            blocks[b] = blocks[b] - column[b] * row
        if j + WINDOW < n:
            ahead[j + WINDOW] = spread(j + WINDOW, (j + 1) // 8)
    rows = [block[:, n:] * lax.rsqrt(p)[:, n:] for block, p in zip(blocks, pivots)]
    return jnp.concatenate(rows, axis=0)


def factor_kernel(packed_ref, start_ref, fibres_ref, out_ref, gram_ref):
    def put(i, j, block):
        gram_ref[i * 128 : (i + 1) * 128, j * 128 : (j + 1) * 128] = block

    row, column = square_indices()
    for own, ((first, second), pairs) in enumerate(SHARES):
        base = own * SHARE_ROWS
        mixed = packed_ref[base : base + 128, :]
        flipped, diagonal = mixed.T, packed_ref[base + 512 : base + 513, :]
        put(first, first, jnp.where(row <= column, mixed, flipped))
        other = jnp.where(row > column, mixed, flipped)
        put(second, second, jnp.where(row == column, diagonal, other))
        for at, (i, j) in enumerate(pairs, 1):
            block = packed_ref[base + at * 128 : base + (at + 1) * 128, :]
            put(i, j, block)
            put(j, i, block.T)
    product = nn(start_ref[...], gram_ref[...], HIGHEST)
    for iteration in range(ITERS):
        small = nt(product, product, HIGHEST)
        if iteration < ITERS - 1:
            product = nn(product, gram_ref[...], HIGHEST)
        product = nn(inverse_cholesky(small), product, HIGHEST)
    core = lax.axis_index("core")
    fibres = jnp.where(core == 0, fibres_ref[0], fibres_ref[1])
    ranked = nn(product.astype(jnp.bfloat16), fibres)
    out_ref[...] = ranked.astype(jnp.bfloat16).astype(jnp.float32)


def unfold_kernel(parts_ref, out_ref):
    chips = parts_ref.shape[0]
    chip = lax.broadcasted_iota(jnp.int32, (chips, 4 * chips), 0)
    station = lax.broadcasted_iota(jnp.int32, (chips, 4 * chips), 1)
    parts = parts_ref[...].astype(jnp.bfloat16)
    out = None
    for at in range(4):
        place = (station == 4 * chip + at).astype(jnp.bfloat16)
        lane = K * (at % 2) + K // 2 * (at // 2)
        term = tn(parts[:, lane : lane + K // 2], place)
        out = term if out is None else out + term
    out_ref[0] = out.astype(jnp.bfloat16)


def swap(array, axes):
    return lax.all_to_all(array, axes, 0, 0, tiled=True)


def from_both_cores(array):
    return lax.all_gather(array, "core", axis=0)


def sum_everywhere(packed):
    shards = 32
    shard = (packed.shape[0] // shards // 2, 2, LANES)
    part = swap(packed.reshape(shards, *shard), PLANE).sum(0)
    part = swap(jnp.broadcast_to(part[None], (8, *shard)), "pair").sum(0)
    return swap(jnp.broadcast_to(part[None], (shards, *shard)), PLANE).reshape(packed.shape)


def per_device(slab, chord_weight, span_weight, start):
    rows, columns = slab.shape[1:]
    tiles = columns // LANES
    inputs = slab, chord_weight, span_weight
    scratch = [
        pltpu.VMEM(slab.shape, slab.dtype),
        pltpu.SMEM(chord_weight.shape, jnp.float32),
        pltpu.SMEM(span_weight.shape, jnp.float32),
        pltpu.SemaphoreType.DMA((3,)),
    ]
    send = call(weigh_kernel, (tiles, rows, LANES), jnp.bfloat16, [HBM] * 3, scratch)(
        *(pltpu.with_memory_space_constraint(array, pltpu.HBM) for array in inputs)
    )
    chips = tiles // 2
    received = swap(send.reshape(chips, 2, rows, LANES), CHIPS)
    received = from_both_cores(received.reshape(tiles * rows, LANES))
    fibres = lax.optimization_barrier(received).reshape(2, chips, 2, rows, LANES)
    fibres = fibres.transpose(2, 1, 0, 3, 4).reshape(2, tiles * rows, LANES)
    share = call(gram_kernel, (SHARE_ROWS, LANES), jnp.float32, [VMEM])(fibres)
    packed = from_both_cores(sum_everywhere(share)).reshape(2 * SHARE_ROWS, LANES)
    chords, rank = start.shape
    parts = call(
        factor_kernel,
        (rank, LANES),
        jnp.float32,
        [VMEM] * 3,
        [pltpu.VMEM((chords, chords), jnp.float32)],
    )(packed, start.T, fibres)
    parts = swap(parts.reshape(rank, 1, LANES), CHIPS).reshape(rank, LANES)
    return call(unfold_kernel, (1, K // 2, 4 * rank), jnp.bfloat16, [VMEM])(parts)


def solution(mesh):
    fine = Mesh(mesh.devices.reshape(4, 8, 2, 2, 4), CHIPS + ("core", "run"))
    return jax.shard_map(
        per_device,
        mesh=fine,
        in_specs=(P("run", CHIPS + ("core",), None), P(CHIPS + ("core",)), P(), P()),
        out_specs=P("run", CHIPS + ("core",), None),
        check_vma=False,
    )
```

```python
import jax
import jax.numpy as jnp
from jax import lax
from jax.experimental import pallas as pl
from jax.experimental.pallas import tpu as pltpu
from jax.sharding import Mesh, PartitionSpec as P

K = 64
ITERS = 3
LANES = 128
WINDOW = 10
HIGHEST = lax.Precision.HIGHEST
VMEM = pl.BlockSpec(memory_space=pltpu.VMEM)
HBM = pl.BlockSpec(memory_space=pltpu.HBM)
CHIPS = ("y", "pair", "side")
PLANE = ("y", "run", "side")
SHARES = [((0, 1), [(0, 1), (0, 2), (0, 3)]), ((2, 3), [(1, 2), (1, 3), (2, 3)])]
SHARE_ROWS = 544


def call(kernel, shape, dtype, specs, scratch=()):
    return pl.pallas_call(
        kernel,
        out_shape=jax.ShapeDtypeStruct(shape, dtype),
        in_specs=specs,
        out_specs=VMEM,
        scratch_shapes=scratch,
        compiler_params=pltpu.CompilerParams(vmem_limit_bytes=32 * 1024 * 1024),
    )


def nn(a, b, precision=None):
    return lax.dot_general(
        a, b, (((1,), (0,)), ((), ())), precision=precision, preferred_element_type=jnp.float32
    )


def nt(a, b, precision=None):
    return lax.dot_general(
        a, b, (((1,), (1,)), ((), ())), precision=precision, preferred_element_type=jnp.float32
    )


def tn(a, b, precision=None):
    return lax.dot_general(
        a, b, (((0,), (0,)), ((), ())), precision=precision, preferred_element_type=jnp.float32
    )


def weigh_kernel(slab_hbm, chord_hbm, span_hbm, out_ref, slab_ref, chord_ref, span_ref, sems):
    copies = [
        pltpu.make_async_copy(slab_hbm, slab_ref, sems.at[0]),
        pltpu.make_async_copy(chord_hbm, chord_ref, sems.at[1]),
        pltpu.make_async_copy(span_hbm, span_ref, sems.at[2]),
    ]
    for copy in copies:
        copy.start()
    for copy in copies[::-1]:
        copy.wait()
    lane = lax.broadcasted_iota(jnp.int32, (1, LANES), 1)
    row = lax.broadcasted_iota(jnp.int32, (out_ref.shape[1], LANES), 0)
    chord = jnp.zeros(row.shape, jnp.float32)
    for i in range(out_ref.shape[1]):
        chord = jnp.where(row == i, chord_ref[i], chord)

    def weigh(tile):
        stations = jnp.where(lane < K, span_ref[2 * tile], span_ref[2 * tile + 1])
        block = slab_ref[0, :, tile * LANES : (tile + 1) * LANES].astype(jnp.float32)
        return block * chord * stations

    low_half = lane % K < K // 2
    for chip in range(out_ref.shape[0] // 2):
        first, second = weigh(2 * chip), weigh(2 * chip + 1)
        low = jnp.where(low_half, first, pltpu.roll(second, K // 2, 1))
        high = jnp.where(low_half, pltpu.roll(first, LANES - K // 2, 1), second)
        out_ref[2 * chip] = low.astype(jnp.bfloat16)
        out_ref[2 * chip + 1] = high.astype(jnp.bfloat16)


def square_indices():
    return (lax.broadcasted_iota(jnp.int32, (128, 128), axis) for axis in range(2))


def gram_kernel(fibres_ref, out_ref):
    core = lax.axis_index("core")

    def block(i, j):
        left, right = pl.ds(i * 128, 128), pl.ds(j * 128, 128)
        return nt(fibres_ref[0, left, :], fibres_ref[0, right, :]) + nt(
            fibres_ref[1, left, :], fibres_ref[1, right, :]
        )

    def make(diagonal, pairs):
        row, column = square_indices()
        first, second = (block(i, i) for i in diagonal)
        out_ref[:128, :] = jnp.where(row <= column, first, second)
        for at, (i, j) in enumerate(pairs, 1):
            out_ref[at * 128 : (at + 1) * 128, :] = block(i, j)
        rest = jnp.sum(jnp.where(row == column, second, 0.0), axis=0, keepdims=True)
        row = row[: SHARE_ROWS - 512]
        out_ref[512:, :] = jnp.where(row == 0, rest, 0.0)

    for own, share in enumerate(SHARES):
        pl.when(core == own)(lambda share=share: make(*share))


def inverse_cholesky(small):
    n = small.shape[0]
    wide = (8, 2 * n)
    eye = lax.broadcasted_iota(jnp.int32, (n, n), 0) == lax.broadcasted_iota(jnp.int32, (n, n), 1)
    both = jnp.concatenate([small, eye.astype(jnp.float32)], axis=1)
    blocks = [both[8 * b : 8 * b + 8] for b in range(n // 8)]
    sub = lax.broadcasted_iota(jnp.int32, wide, 0)

    def spread(column, since):
        return {
            b: jnp.broadcast_to(blocks[b][:, column : column + 1], wide)
            for b in range(since, n // 8)
        }

    ahead = {column: spread(column, 0) for column in range(WINDOW)}
    pivots = [None] * (n // 8)
    for j in range(n):
        own, k = divmod(j, 8)
        column = ahead.pop(j)
        pivot = jnp.broadcast_to(column[own][k : k + 1], wide)
        pivots[own] = pivot if k == 0 else jnp.where(sub >= k, pivot, pivots[own])
        inverse = 1.0 / pivot
        row = jnp.broadcast_to(blocks[own][k : k + 1], wide) * inverse
        column[own] = jnp.where(sub > k, column[own], 0.0)
        for later in ahead.values():
            scale = jnp.broadcast_to(later[own][k : k + 1], wide) * inverse
            for b in range(own, n // 8):
                later[b] = later[b] - column[b] * scale
        for b in range(own, n // 8):
            blocks[b] = blocks[b] - column[b] * row
        if j + WINDOW < n:
            ahead[j + WINDOW] = spread(j + WINDOW, (j + 1) // 8)
    rows = [block[:, n:] * lax.rsqrt(p)[:, n:] for block, p in zip(blocks, pivots)]
    return jnp.concatenate(rows, axis=0)


def factor_kernel(packed_ref, start_ref, fibres_ref, out_ref, gram_ref):
    def put(i, j, block):
        gram_ref[i * 128 : (i + 1) * 128, j * 128 : (j + 1) * 128] = block

    row, column = square_indices()
    for own, ((first, second), pairs) in enumerate(SHARES):
        base = own * SHARE_ROWS
        mixed = packed_ref[base : base + 128, :]
        flipped, diagonal = mixed.T, packed_ref[base + 512 : base + 513, :]
        put(first, first, jnp.where(row <= column, mixed, flipped))
        other = jnp.where(row > column, mixed, flipped)
        put(second, second, jnp.where(row == column, diagonal, other))
        for at, (i, j) in enumerate(pairs, 1):
            block = packed_ref[base + at * 128 : base + (at + 1) * 128, :]
            put(i, j, block)
            put(j, i, block.T)
    product = nn(start_ref[...], gram_ref[...], HIGHEST)
    for iteration in range(ITERS):
        small = nt(product, product, HIGHEST)
        if iteration < ITERS - 1:
            product = nn(product, gram_ref[...], HIGHEST)
        product = nn(inverse_cholesky(small), product, HIGHEST)
    core = lax.axis_index("core")
    fibres = jnp.where(core == 0, fibres_ref[0], fibres_ref[1])
    ranked = nn(product.astype(jnp.bfloat16), fibres)
    out_ref[...] = ranked.astype(jnp.bfloat16).astype(jnp.float32)


def unfold_kernel(parts_ref, out_ref):
    chips = parts_ref.shape[0]
    chip = lax.broadcasted_iota(jnp.int32, (chips, 4 * chips), 0)
    station = lax.broadcasted_iota(jnp.int32, (chips, 4 * chips), 1)
    parts = parts_ref[...].astype(jnp.bfloat16)
    out = None
    for at in range(4):
        place = (station == 4 * chip + at).astype(jnp.bfloat16)
        lane = K * (at % 2) + K // 2 * (at // 2)
        term = tn(parts[:, lane : lane + K // 2], place)
        out = term if out is None else out + term
    out_ref[0] = out.astype(jnp.bfloat16)


def swap(array, axes):
    return lax.all_to_all(array, axes, 0, 0, tiled=True)


def from_both_cores(array):
    return lax.all_gather(array, "core", axis=0)


def sum_everywhere(packed):
    shards = 32
    shard = (packed.shape[0] // shards, 1, LANES)
    part = swap(packed.reshape(shards, *shard), PLANE).sum(0)
    part = swap(jnp.broadcast_to(part[None], (8, *shard)), "pair").sum(0)
    return swap(jnp.broadcast_to(part[None], (shards, *shard)), PLANE).reshape(packed.shape)


def per_device(slab, chord_weight, span_weight, start):
    rows, columns = slab.shape[1:]
    tiles = columns // LANES
    inputs = slab, chord_weight, span_weight
    scratch = [
        pltpu.VMEM(slab.shape, slab.dtype),
        pltpu.SMEM(chord_weight.shape, jnp.float32),
        pltpu.SMEM(span_weight.shape, jnp.float32),
        pltpu.SemaphoreType.DMA((3,)),
    ]
    send = call(weigh_kernel, (tiles, rows, LANES), jnp.bfloat16, [HBM] * 3, scratch)(
        *(pltpu.with_memory_space_constraint(array, pltpu.HBM) for array in inputs)
    )
    chips = tiles // 2
    received = swap(send.reshape(chips, 2, rows, LANES), CHIPS)
    received = from_both_cores(received.reshape(tiles * rows, LANES))
    fibres = lax.optimization_barrier(received).reshape(2, chips, 2, rows, LANES)
    fibres = fibres.transpose(2, 1, 0, 3, 4).reshape(2, tiles * rows, LANES)
    share = call(gram_kernel, (SHARE_ROWS, LANES), jnp.float32, [VMEM])(fibres)
    packed = from_both_cores(sum_everywhere(share)).reshape(2 * SHARE_ROWS, LANES)
    chords, rank = start.shape
    parts = call(
        factor_kernel,
        (rank, LANES),
        jnp.float32,
        [VMEM] * 3,
        [pltpu.VMEM((chords, chords), jnp.float32)],
    )(packed, start.T, fibres)
    parts = swap(parts.reshape(rank, 1, LANES), CHIPS).reshape(rank, LANES)
    return call(unfold_kernel, (1, K // 2, 4 * rank), jnp.bfloat16, [VMEM])(parts)


def solution(mesh):
    fine = Mesh(mesh.devices.reshape(4, 8, 2, 2, 4), CHIPS + ("core", "run"))
    return jax.shard_map(
        per_device,
        mesh=fine,
        in_specs=(P("run", CHIPS + ("core",), None), P(CHIPS + ("core",)), P(), P()),
        out_specs=P("run", CHIPS + ("core",), None),
        check_vma=False,
    )
```

```python
import jax
import jax.numpy as jnp
from jax import lax
from jax.experimental import pallas as pl
from jax.experimental.pallas import tpu as pltpu
from jax.sharding import Mesh, PartitionSpec as P

K = 64
ITERS = 3
LANES = 128
WINDOW = 10
HIGHEST = lax.Precision.HIGHEST
VMEM = pl.BlockSpec(memory_space=pltpu.VMEM)
HBM = pl.BlockSpec(memory_space=pltpu.HBM)
CHIPS = ("y", "pair", "side")
PLANE = ("y", "run", "side")
SHARES = [((0, 1), [(0, 1), (0, 2), (0, 3)]), ((2, 3), [(1, 2), (1, 3), (2, 3)])]
SHARE_ROWS = 544


def call(kernel, shape, dtype, specs, scratch=()):
    return pl.pallas_call(
        kernel,
        out_shape=jax.ShapeDtypeStruct(shape, dtype),
        in_specs=specs,
        out_specs=VMEM,
        scratch_shapes=scratch,
        compiler_params=pltpu.CompilerParams(vmem_limit_bytes=32 * 1024 * 1024),
    )


def nn(a, b, precision=None):
    return lax.dot_general(
        a, b, (((1,), (0,)), ((), ())), precision=precision, preferred_element_type=jnp.float32
    )


def nt(a, b, precision=None):
    return lax.dot_general(
        a, b, (((1,), (1,)), ((), ())), precision=precision, preferred_element_type=jnp.float32
    )


def tn(a, b, precision=None):
    return lax.dot_general(
        a, b, (((0,), (0,)), ((), ())), precision=precision, preferred_element_type=jnp.float32
    )


def weigh_kernel(slab_hbm, chord_hbm, span_hbm, out_ref, slab_ref, chord_ref, span_ref, sems):
    copies = [
        pltpu.make_async_copy(slab_hbm, slab_ref, sems.at[0]),
        pltpu.make_async_copy(chord_hbm, chord_ref, sems.at[1]),
        pltpu.make_async_copy(span_hbm, span_ref, sems.at[2]),
    ]
    for copy in copies:
        copy.start()
    for copy in copies[::-1]:
        copy.wait()
    lane = lax.broadcasted_iota(jnp.int32, (1, LANES), 1)
    row = lax.broadcasted_iota(jnp.int32, (out_ref.shape[1], LANES), 0)
    chord = jnp.zeros(row.shape, jnp.float32)
    for i in range(out_ref.shape[1]):
        chord = jnp.where(row == i, chord_ref[i], chord)

    def weigh(tile):
        stations = jnp.where(lane < K, span_ref[2 * tile], span_ref[2 * tile + 1])
        block = slab_ref[0, :, tile * LANES : (tile + 1) * LANES].astype(jnp.float32)
        return block * chord * stations

    low_half = lane % K < K // 2
    for chip in range(out_ref.shape[0] // 2):
        first, second = weigh(2 * chip), weigh(2 * chip + 1)
        turned = pltpu.roll(jnp.where(low_half, second, first), K // 2, 1)
        low = jnp.where(low_half, first, turned)
        high = jnp.where(low_half, turned, second)
        out_ref[2 * chip] = low.astype(jnp.bfloat16)
        out_ref[2 * chip + 1] = high.astype(jnp.bfloat16)


def square_indices():
    return (lax.broadcasted_iota(jnp.int32, (128, 128), axis) for axis in range(2))


def gram_kernel(fibres_ref, out_ref):
    core = lax.axis_index("core")

    def block(i, j):
        left, right = pl.ds(i * 128, 128), pl.ds(j * 128, 128)
        return nt(fibres_ref[0, left, :], fibres_ref[0, right, :]) + nt(
            fibres_ref[1, left, :], fibres_ref[1, right, :]
        )

    def make(diagonal, pairs):
        row, column = square_indices()
        first, second = (block(i, i) for i in diagonal)
        out_ref[:128, :] = jnp.where(row <= column, first, second)
        for at, (i, j) in enumerate(pairs, 1):
            out_ref[at * 128 : (at + 1) * 128, :] = block(i, j)
        rest = jnp.sum(jnp.where(row == column, second, 0.0), axis=0, keepdims=True)
        row = row[: SHARE_ROWS - 512]
        out_ref[512:, :] = jnp.where(row == 0, rest, 0.0)

    for own, share in enumerate(SHARES):
        pl.when(core == own)(lambda share=share: make(*share))


def inverse_cholesky(small):
    n = small.shape[0]
    wide = (8, 2 * n)
    eye = lax.broadcasted_iota(jnp.int32, (n, n), 0) == lax.broadcasted_iota(jnp.int32, (n, n), 1)
    both = jnp.concatenate([small, eye.astype(jnp.float32)], axis=1)
    blocks = [both[8 * b : 8 * b + 8] for b in range(n // 8)]
    sub = lax.broadcasted_iota(jnp.int32, wide, 0)

    def spread(column, since):
        return {
            b: jnp.broadcast_to(blocks[b][:, column : column + 1], wide)
            for b in range(since, n // 8)
        }

    ahead = {column: spread(column, 0) for column in range(WINDOW)}
    pivots = [None] * (n // 8)
    for j in range(n):
        own, k = divmod(j, 8)
        column = ahead.pop(j)
        pivot = jnp.broadcast_to(column[own][k : k + 1], wide)
        pivots[own] = pivot if k == 0 else jnp.where(sub >= k, pivot, pivots[own])
        inverse = 1.0 / pivot
        row = jnp.broadcast_to(blocks[own][k : k + 1], wide) * inverse
        column[own] = jnp.where(sub > k, column[own], 0.0)
        for later in ahead.values():
            scale = jnp.broadcast_to(later[own][k : k + 1], wide) * inverse
            for b in range(own, n // 8):
                later[b] = later[b] - column[b] * scale
        for b in range(own, n // 8):
            blocks[b] = blocks[b] - column[b] * row
        if j + WINDOW < n:
            ahead[j + WINDOW] = spread(j + WINDOW, (j + 1) // 8)
    rows = [block[:, n:] * lax.rsqrt(p)[:, n:] for block, p in zip(blocks, pivots)]
    return jnp.concatenate(rows, axis=0)


def factor_kernel(packed_ref, start_ref, fibres_ref, out_ref, gram_ref):
    def put(i, j, block):
        gram_ref[i * 128 : (i + 1) * 128, j * 128 : (j + 1) * 128] = block

    row, column = square_indices()
    for own, ((first, second), pairs) in enumerate(SHARES):
        base = own * SHARE_ROWS
        mixed = packed_ref[base : base + 128, :]
        flipped, diagonal = mixed.T, packed_ref[base + 512 : base + 513, :]
        put(first, first, jnp.where(row <= column, mixed, flipped))
        other = jnp.where(row > column, mixed, flipped)
        put(second, second, jnp.where(row == column, diagonal, other))
        for at, (i, j) in enumerate(pairs, 1):
            block = packed_ref[base + at * 128 : base + (at + 1) * 128, :]
            put(i, j, block)
            put(j, i, block.T)
    product = nn(start_ref[...], gram_ref[...], HIGHEST)
    for iteration in range(ITERS):
        small = nt(product, product, HIGHEST)
        if iteration < ITERS - 1:
            product = nn(product, gram_ref[...], HIGHEST)
        product = nn(inverse_cholesky(small), product, HIGHEST)
    core = lax.axis_index("core")
    fibres = jnp.where(core == 0, fibres_ref[0], fibres_ref[1])
    ranked = nn(product.astype(jnp.bfloat16), fibres)
    out_ref[...] = ranked.astype(jnp.bfloat16).astype(jnp.float32)


def unfold_kernel(parts_ref, out_ref):
    chips = parts_ref.shape[0]
    chip = lax.broadcasted_iota(jnp.int32, (chips, 4 * chips), 0)
    station = lax.broadcasted_iota(jnp.int32, (chips, 4 * chips), 1)
    parts = parts_ref[...].astype(jnp.bfloat16)
    core = lax.axis_index("core")
    out = None
    for at in range(4):
        which = jnp.where(core == 0, at, 1 - at) if at < 2 else at
        place = (station == 4 * chip + which).astype(jnp.bfloat16)
        lane = K * (at % 2) + K // 2 * (at // 2)
        term = tn(parts[:, lane : lane + K // 2], place)
        out = term if out is None else out + term
    out_ref[0] = out.astype(jnp.bfloat16)


def swap(array, axes):
    return lax.all_to_all(array, axes, 0, 0, tiled=True)


def from_both_cores(array):
    return lax.all_gather(array, "core", axis=0)


def sum_everywhere(packed):
    shards = 32
    shard = (packed.shape[0] // shards, 1, LANES)
    part = swap(packed.reshape(shards, *shard), PLANE).sum(0)
    part = swap(jnp.broadcast_to(part[None], (8, *shard)), "pair").sum(0)
    return swap(jnp.broadcast_to(part[None], (shards, *shard)), PLANE).reshape(packed.shape)


def per_device(slab, chord_weight, span_weight, start):
    rows, columns = slab.shape[1:]
    tiles = columns // LANES
    inputs = slab, chord_weight, span_weight
    scratch = [
        pltpu.VMEM(slab.shape, slab.dtype),
        pltpu.SMEM(chord_weight.shape, jnp.float32),
        pltpu.SMEM(span_weight.shape, jnp.float32),
        pltpu.SemaphoreType.DMA((3,)),
    ]
    send = call(weigh_kernel, (tiles, rows, LANES), jnp.bfloat16, [HBM] * 3, scratch)(
        *(pltpu.with_memory_space_constraint(array, pltpu.HBM) for array in inputs)
    )
    chips = tiles // 2
    received = swap(send.reshape(chips, 2, rows, LANES), CHIPS)
    received = from_both_cores(received.reshape(tiles * rows, LANES))
    fibres = lax.optimization_barrier(received).reshape(2, chips, 2, rows, LANES)
    fibres = fibres.transpose(2, 1, 0, 3, 4).reshape(2, tiles * rows, LANES)
    share = call(gram_kernel, (SHARE_ROWS, LANES), jnp.float32, [VMEM])(fibres)
    packed = from_both_cores(sum_everywhere(share)).reshape(2 * SHARE_ROWS, LANES)
    chords, rank = start.shape
    parts = call(
        factor_kernel,
        (rank, LANES),
        jnp.float32,
        [VMEM] * 3,
        [pltpu.VMEM((chords, chords), jnp.float32)],
    )(packed, start.T, fibres)
    parts = swap(parts.reshape(rank, 1, LANES), CHIPS).reshape(rank, LANES)
    return call(unfold_kernel, (1, K // 2, 4 * rank), jnp.bfloat16, [VMEM])(parts)


def solution(mesh):
    fine = Mesh(mesh.devices.reshape(4, 8, 2, 2, 4), CHIPS + ("core", "run"))
    return jax.shard_map(
        per_device,
        mesh=fine,
        in_specs=(P("run", CHIPS + ("core",), None), P(CHIPS + ("core",)), P(), P()),
        out_specs=P("run", CHIPS + ("core",), None),
        check_vma=False,
    )
```

```python
import jax
import jax.numpy as jnp
from jax import lax
from jax.experimental import pallas as pl
from jax.experimental.pallas import tpu as pltpu
from jax.sharding import Mesh, PartitionSpec as P

K = 64
ITERS = 3
LANES = 128
WINDOW = 10
HIGHEST = lax.Precision.HIGHEST
VMEM = pl.BlockSpec(memory_space=pltpu.VMEM)
HBM = pl.BlockSpec(memory_space=pltpu.HBM)
CHIPS = ("y", "pair", "side")
PLANE = ("y", "run", "side")
SHARES = [((0, 1), [(0, 1), (0, 2), (0, 3)]), ((2, 3), [(1, 2), (1, 3), (2, 3)])]
SHARE_ROWS = 544


def call(kernel, shape, dtype, specs, scratch=()):
    return pl.pallas_call(
        kernel,
        out_shape=jax.ShapeDtypeStruct(shape, dtype),
        in_specs=specs,
        out_specs=VMEM,
        scratch_shapes=scratch,
        compiler_params=pltpu.CompilerParams(vmem_limit_bytes=32 * 1024 * 1024),
    )


def nn(a, b, precision=None):
    return lax.dot_general(
        a, b, (((1,), (0,)), ((), ())), precision=precision, preferred_element_type=jnp.float32
    )


def nt(a, b, precision=None):
    return lax.dot_general(
        a, b, (((1,), (1,)), ((), ())), precision=precision, preferred_element_type=jnp.float32
    )


def tn(a, b, precision=None):
    return lax.dot_general(
        a, b, (((0,), (0,)), ((), ())), precision=precision, preferred_element_type=jnp.float32
    )


def weigh_kernel(slab_hbm, chord_hbm, span_hbm, out_ref, slab_ref, chord_ref, span_ref, sems):
    copies = [
        pltpu.make_async_copy(slab_hbm, slab_ref, sems.at[0]),
        pltpu.make_async_copy(chord_hbm, chord_ref, sems.at[1]),
        pltpu.make_async_copy(span_hbm, span_ref, sems.at[2]),
    ]
    for copy in copies:
        copy.start()
    for copy in copies[::-1]:
        copy.wait()
    lane = lax.broadcasted_iota(jnp.int32, (1, LANES), 1)
    row = lax.broadcasted_iota(jnp.int32, (out_ref.shape[1], LANES), 0)
    chord = jnp.zeros(row.shape, jnp.float32)
    for i in range(out_ref.shape[1]):
        chord = jnp.where(row == i, chord_ref[i], chord)

    def weigh(tile):
        stations = jnp.where(lane < K, span_ref[2 * tile], span_ref[2 * tile + 1])
        block = slab_ref[0, :, tile * LANES : (tile + 1) * LANES].astype(jnp.float32)
        return block * chord * stations

    low_half = lane % K < K // 2
    for chip in range(out_ref.shape[0] // 2):
        first, second = weigh(2 * chip), weigh(2 * chip + 1)
        low = jnp.where(low_half, first, pltpu.roll(second, K // 2, 1))
        high = jnp.where(low_half, pltpu.roll(first, LANES - K // 2, 1), second)
        out_ref[2 * chip] = low.astype(jnp.bfloat16)
        out_ref[2 * chip + 1] = high.astype(jnp.bfloat16)


def square_indices():
    return (lax.broadcasted_iota(jnp.int32, (128, 128), axis) for axis in range(2))


def gram_kernel(fibres_ref, out_ref):
    core = lax.axis_index("core")

    def block(i, j):
        left, right = pl.ds(i * 128, 128), pl.ds(j * 128, 128)
        return nt(fibres_ref[0, left, :], fibres_ref[0, right, :]) + nt(
            fibres_ref[1, left, :], fibres_ref[1, right, :]
        )

    def make(diagonal, pairs):
        row, column = square_indices()
        first, second = (block(i, i) for i in diagonal)
        out_ref[:128, :] = jnp.where(row <= column, first, second)
        for at, (i, j) in enumerate(pairs, 1):
            out_ref[at * 128 : (at + 1) * 128, :] = block(i, j)
        rest = jnp.sum(jnp.where(row == column, second, 0.0), axis=0, keepdims=True)
        row = row[: SHARE_ROWS - 512]
        out_ref[512:, :] = jnp.where(row == 0, rest, 0.0)

    for own, share in enumerate(SHARES):
        pl.when(core == own)(lambda share=share: make(*share))


def inverse_cholesky(small):
    n = small.shape[0]
    wide = (8, 2 * n)
    eye = lax.broadcasted_iota(jnp.int32, (n, n), 0) == lax.broadcasted_iota(jnp.int32, (n, n), 1)
    both = jnp.concatenate([small, eye.astype(jnp.float32)], axis=1)
    blocks = [both[8 * b : 8 * b + 8] for b in range(n // 8)]
    sub = lax.broadcasted_iota(jnp.int32, wide, 0)

    def spread(column, since):
        return {
            b: jnp.broadcast_to(blocks[b][:, column : column + 1], wide)
            for b in range(since, n // 8)
        }

    ahead = {column: spread(column, 0) for column in range(WINDOW)}
    pivots = [None] * (n // 8)
    for j in range(n):
        own, k = divmod(j, 8)
        column = ahead.pop(j)
        pivot = jnp.broadcast_to(column[own][k : k + 1], wide)
        pivots[own] = pivot if k == 0 else jnp.where(sub >= k, pivot, pivots[own])
        inverse = 1.0 / pivot
        row = jnp.broadcast_to(blocks[own][k : k + 1], wide) * inverse
        column[own] = jnp.where(sub > k, column[own], 0.0)
        for later in ahead.values():
            scale = jnp.broadcast_to(later[own][k : k + 1], wide) * inverse
            for b in range(own, n // 8):
                later[b] = later[b] - column[b] * scale
        for b in range(own, n // 8):
            blocks[b] = blocks[b] - column[b] * row
        if j + WINDOW < n:
            ahead[j + WINDOW] = spread(j + WINDOW, (j + 1) // 8)
    rows = [block[:, n:] * lax.rsqrt(p)[:, n:] for block, p in zip(blocks, pivots)]
    return jnp.concatenate(rows, axis=0)


def with_itself(a):
    high = a.astype(jnp.bfloat16)
    rest = a - high.astype(jnp.float32)
    middle = rest.astype(jnp.bfloat16)
    low = (rest - middle.astype(jnp.float32)).astype(jnp.bfloat16)
    mirrored = nt(low, high) + nt(middle, high)
    return (mirrored + mirrored.T) + nt(middle, middle) + nt(high, high)


def factor_kernel(packed_ref, start_ref, fibres_ref, out_ref, gram_ref):
    def put(i, j, block):
        gram_ref[i * 128 : (i + 1) * 128, j * 128 : (j + 1) * 128] = block

    row, column = square_indices()
    for own, ((first, second), pairs) in enumerate(SHARES):
        base = own * SHARE_ROWS
        mixed = packed_ref[base : base + 128, :]
        flipped, diagonal = mixed.T, packed_ref[base + 512 : base + 513, :]
        put(first, first, jnp.where(row <= column, mixed, flipped))
        other = jnp.where(row > column, mixed, flipped)
        put(second, second, jnp.where(row == column, diagonal, other))
        for at, (i, j) in enumerate(pairs, 1):
            block = packed_ref[base + at * 128 : base + (at + 1) * 128, :]
            put(i, j, block)
            put(j, i, block.T)
    product = nn(start_ref[...], gram_ref[...], HIGHEST)
    for iteration in range(ITERS):
        small = with_itself(product)
        if iteration < ITERS - 1:
            product = nn(product, gram_ref[...], HIGHEST)
        product = nn(inverse_cholesky(small), product, HIGHEST)
    core = lax.axis_index("core")
    fibres = jnp.where(core == 0, fibres_ref[0], fibres_ref[1])
    ranked = nn(product.astype(jnp.bfloat16), fibres)
    out_ref[...] = ranked.astype(jnp.bfloat16).astype(jnp.float32)


def unfold_kernel(parts_ref, out_ref):
    chips = parts_ref.shape[0]
    chip = lax.broadcasted_iota(jnp.int32, (chips, 4 * chips), 0)
    station = lax.broadcasted_iota(jnp.int32, (chips, 4 * chips), 1)
    parts = parts_ref[...].astype(jnp.bfloat16)
    out = None
    for at in range(4):
        place = (station == 4 * chip + at).astype(jnp.bfloat16)
        lane = K * (at % 2) + K // 2 * (at // 2)
        term = tn(parts[:, lane : lane + K // 2], place)
        out = term if out is None else out + term
    out_ref[0] = out.astype(jnp.bfloat16)


def swap(array, axes):
    return lax.all_to_all(array, axes, 0, 0, tiled=True)


def from_both_cores(array):
    return lax.all_gather(array, "core", axis=0)


def sum_everywhere(packed):
    shards = 32
    shard = (packed.shape[0] // shards, 1, LANES)
    part = swap(packed.reshape(shards, *shard), PLANE).sum(0)
    part = swap(jnp.broadcast_to(part[None], (8, *shard)), "pair").sum(0)
    return swap(jnp.broadcast_to(part[None], (shards, *shard)), PLANE).reshape(packed.shape)


def per_device(slab, chord_weight, span_weight, start):
    rows, columns = slab.shape[1:]
    tiles = columns // LANES
    inputs = slab, chord_weight, span_weight
    scratch = [
        pltpu.VMEM(slab.shape, slab.dtype),
        pltpu.SMEM(chord_weight.shape, jnp.float32),
        pltpu.SMEM(span_weight.shape, jnp.float32),
        pltpu.SemaphoreType.DMA((3,)),
    ]
    send = call(weigh_kernel, (tiles, rows, LANES), jnp.bfloat16, [HBM] * 3, scratch)(
        *(pltpu.with_memory_space_constraint(array, pltpu.HBM) for array in inputs)
    )
    chips = tiles // 2
    received = swap(send.reshape(chips, 2, rows, LANES), CHIPS)
    received = from_both_cores(received.reshape(tiles * rows, LANES))
    fibres = lax.optimization_barrier(received).reshape(2, chips, 2, rows, LANES)
    fibres = fibres.transpose(2, 1, 0, 3, 4).reshape(2, tiles * rows, LANES)
    share = call(gram_kernel, (SHARE_ROWS, LANES), jnp.float32, [VMEM])(fibres)
    packed = from_both_cores(sum_everywhere(share)).reshape(2 * SHARE_ROWS, LANES)
    chords, rank = start.shape
    parts = call(
        factor_kernel,
        (rank, LANES),
        jnp.float32,
        [VMEM] * 3,
        [pltpu.VMEM((chords, chords), jnp.float32)],
    )(packed, start.T, fibres)
    parts = swap(parts.reshape(rank, 1, LANES), CHIPS).reshape(rank, LANES)
    return call(unfold_kernel, (1, K // 2, 4 * rank), jnp.bfloat16, [VMEM])(parts)


def solution(mesh):
    fine = Mesh(mesh.devices.reshape(4, 8, 2, 2, 4), CHIPS + ("core", "run"))
    return jax.shard_map(
        per_device,
        mesh=fine,
        in_specs=(P("run", CHIPS + ("core",), None), P(CHIPS + ("core",)), P(), P()),
        out_specs=P("run", CHIPS + ("core",), None),
        check_vma=False,
    )
```
